512 devices in a mesh: dist: 4 (over y_hi, core), tile: 128 (over y_lo, x, z).
Axes of the slice: x: 4, y: 4 (y_hi: 2, y_lo: 2; y = y_hi * 2 + y_lo), z: 16, core: 2. Of those that a mesh axis runs over, the one named last changes fastest.
Arguments:
- object_re: float32 [16384, 128], P('tile'), may hold values from -6 to 6
- object_im: float32 [16384, 128], P('tile'), may hold values from -6 to 6
- intensity: float32 [4, 16384, 128], P('dist', 'tile'), may hold values from 0.25 to 4
- shrink: int32 [4], P('dist'), may hold values from 32 to 64, as said below
- offset: int32 [4], P('dist'), may hold values from -31 to 31, as said below
- fresnel: int32 [4], P('dist'), may hold values from 4 to 16
Outputs:
- gradient_re: float32 [16384, 128], P('tile')
- gradient_im: float32 [16384, 128], P('tile')
The draws below stay inside these ranges and needn't reach their ends.
Inputs may be any that keep to these rules, and one draw needn't show every extreme that they name: `shrink`: some distance has the largest value; the distances that take the two extreme offsets have the smallest. `offset`: both extreme values occur, at two different distances.
All inputs are finite; a program needn't handle non-finite values.
Results may differ from the reference program's by a relative error of at most 0.0003.
Values sent between devices are 32-bit elements; how exact they have to be, the bound alone decides.
No kernel may reach another device: no remote copies, remote signals or barrier semaphores. Data moves between devices by JAX's collectives and lax.ppermute only.
A program may use at most 128 MiB of HBM per device.

```python
import math
import jax
import jax.numpy as jnp
from jax import lax

ROWS_DEV = 128
COLS = 128
NROWS = 16384
HALO = 64
DIST = 4


def distance_roles(key):
    role_key = jax.random.fold_in(key, 5)
    return jax.random.permutation(role_key, DIST).astype(jnp.int32)


def draw_shrink(key, part):
    roles = distance_roles(key)
    key = jax.random.fold_in(key, 11)
    values = jax.random.randint(key, (DIST,), ROWS_DEV // 4, ROWS_DEV // 2 + 1, dtype=jnp.int32)
    places = jnp.arange(DIST, dtype=jnp.int32)
    values = jnp.where(places == roles[0], ROWS_DEV // 2, values)
    values = jnp.where(places == roles[1], ROWS_DEV // 4, values)
    values = jnp.where(places == roles[2], ROWS_DEV // 4, values)
    return values.astype(jnp.int32)


def draw_offset(key, part):
    roles = distance_roles(key)
    key = jax.random.fold_in(key, 23)
    reach = ROWS_DEV // 4 - 1
    values = jax.random.randint(key, (DIST,), -reach, reach + 1, dtype=jnp.int32)
    places = jnp.arange(DIST, dtype=jnp.int32)
    values = jnp.where(places == roles[1], -reach, values)
    values = jnp.where(places == roles[2], reach, values)
    return values.astype(jnp.int32)


def set_ends(result, stream_key, smallest, largest):
    place = [jax.random.randint(jax.random.fold_in(stream_key, axis), (), 0, length) for axis, length in enumerate(result.shape)]
    main_axis = result.shape.index(max(result.shape))
    beside = place[:main_axis] + [(place[main_axis] + 1) % result.shape[main_axis]] + place[main_axis + 1:]
    return result.at[tuple(place)].set(smallest).at[tuple(beside)].set(largest)


def levels(rng, dims, pieces, low, largest):
    def one(axis_at, shards_of):
        steps = jax.random.uniform(jax.random.fold_in(jax.random.fold_in(rng, 6), axis_at), (shards_of,), jnp.float32, low / len(pieces), largest / len(pieces))
        return jnp.repeat(jnp.exp(steps), dims[axis_at] // shards_of).reshape((-1,) + (1,) * (len(dims) - axis_at - 1))

    level = one(*pieces[0])
    for cut in pieces[1:]:
        level = level * one(*cut)
    return level


def normal_values(own_key, extent, width, most, split=(), kind=jnp.bfloat16):
    values = jax.random.normal(own_key, extent, jnp.float32) * width
    if len(split) > 0:
        values = levels(own_key, extent, split, -0.22, 0.18) * values
    return jnp.clip(values, min=-most, max=most).astype(kind)


def setup_inputs(seed: int = 0) -> dict:
    key_list = jax.random.split(jax.random.key(seed), 7)
    object_re = normal_values(key_list[0], (NROWS, COLS), 0.7, 6.0, ((0, 128),), jnp.float32)
    object_im = normal_values(key_list[1], (NROWS, COLS), 0.7, 6.0, ((0, 128),), jnp.float32)
    intensity = jnp.clip(jnp.exp(math.log(4.0) - 2.7725887 * jax.random.uniform(key_list[2], (DIST, NROWS, COLS), jnp.float32) ** levels(key_list[2], (DIST, NROWS, COLS), ((0, 4), (1, 128)), -0.2, 0.2)), 0.25, 4.0)
    shrink = draw_shrink(jax.random.fold_in(key_list[6], 71), 0)
    offset = draw_offset(jax.random.fold_in(key_list[6], 71), 0)
    fresnel = set_ends(jax.random.randint(key_list[5], (DIST,), 4, 17), jax.random.fold_in(key_list[5], 1), 4, 16).astype(jnp.int32)
    return {"object_re": object_re, "object_im": object_im, "intensity": intensity, "shrink": shrink, "offset": offset, "fresnel": fresnel}


def reference(object_re, object_im, intensity, shrink, offset, fresnel):
    row_total = NROWS
    period = 64 * row_total
    object_field = lax.complex(object_re, object_im)
    indices = jnp.arange(row_total, dtype=jnp.int32)
    padded = jnp.pad(object_field, ((HALO, HALO), (0, 0)))
    signed = jnp.where(indices < row_total // 2, indices, indices - row_total)
    square = signed * signed % period
    gradient = jnp.zeros((row_total + 2 * HALO, COLS), object_field.dtype)
    for distance in range(DIST):
        scaled = row_total // 2 * row_total + (indices - row_total // 2) * (row_total - shrink[distance]) + offset[distance] * row_total
        lower = (jnp.floor_divide(scaled, row_total) + HALO).astype(jnp.int32)
        weight = (jnp.remainder(scaled, row_total).astype(jnp.float32) / row_total)[:, None]
        sampled = (1.0 - weight) * padded[lower] + weight * padded[lower + 1]
        turns = fresnel[distance] * square % period
        theta = 2.0 * math.pi / period * turns.astype(jnp.float32)
        kernel = lax.complex(jnp.cos(theta), -jnp.sin(theta))[:, None]
        wave = jnp.fft.ifft(jnp.fft.fft(sampled, axis=0) * kernel, axis=0)
        magnitude = jnp.abs(wave)
        ratio = jnp.sqrt(intensity[distance]) / jnp.maximum(magnitude, 0.1)
        residual = wave - ratio * wave
        back_wave = jnp.fft.ifft(jnp.fft.fft(residual, axis=0) * jnp.conj(kernel), axis=0)
        gradient = gradient.at[lower].add((1.0 - weight) * back_wave)
        gradient = gradient.at[lower + 1].add(weight * back_wave)
    gradient = gradient[HALO:HALO + row_total]
    return (jnp.real(gradient).astype(jnp.float32), jnp.imag(gradient).astype(jnp.float32))
```

```python
from functools import partial
import math

import jax
import jax.numpy as jnp
import numpy as np
from jax import lax
from jax.experimental import pallas as pl
from jax.experimental.pallas import tpu as pltpu
from jax.sharding import PartitionSpec as P

F32 = jnp.float32
BF16 = jnp.bfloat16


def two_terms(values):
    high = values.astype(BF16)
    low = (values - high.astype(np.float32)).astype(BF16)
    return high, low


def constant_tables(size):
    index = np.arange(size, dtype=np.int64)
    product = np.outer(index, index)
    angle = 2.0 * np.pi / size * (product % size)
    real, imag = np.cos(angle), -np.sin(angle)
    block = np.block([[real, -imag], [imag, real]]).astype(np.float32)
    angle = 2.0 * np.pi / (size * size) * product
    twiddle = np.stack([np.cos(angle), -np.sin(angle)]).astype(np.float32)
    return two_terms(block) + (twiddle,)


def split(values):
    high = values.astype(BF16)
    return high, (values - high.astype(F32)).astype(BF16)


def product(left, right):
    dot = partial(jnp.dot, preferred_element_type=F32)
    return dot(left[0], right[0]) + (dot(left[0], right[1]) + dot(left[1], right[0]))


def times(first, second):
    return (
        first[0] * second[0] - first[1] * second[1],
        first[0] * second[1] + first[1] * second[0],
    )


def conj(pair):
    return (pair[0], -pair[1])


def propagate(values, block, block_t, twiddle, kernel, size):
    def by_rows(table, pair):
        out = product(table, split(jnp.concatenate(pair, axis=0)))
        return (out[:size], out[size:])

    def by_lanes(pair, table):
        out = product(split(jnp.concatenate(pair, axis=1)), table)
        return (out[:, :size], out[:, size:])

    mixed = times(by_rows(block, values), twiddle)
    spectrum = times(by_lanes(mixed, block_t), kernel)
    mixed = times(by_lanes(spectrum, block), conj(twiddle))
    return by_rows(block_t, mixed)


def column_kernel(size, scalars, field_ref, phase_ref, high_ref, low_ref, high_t_ref, low_t_ref, twiddle_ref, out_ref):
    shape = (size, size)
    row = lax.broadcasted_iota(jnp.int32, shape, 0)
    lane = lax.broadcasted_iota(jnp.int32, shape, 1)
    total = size * size
    bits = total.bit_length() - 1
    shrink, offset = scalars[0], scalars[1]

    def scaled(index):
        centre = total // 2
        return centre * total + (index - centre) * (total - shrink) + offset * total

    place = scaled(row * size + lane)
    weight = jnp.bitwise_and(place, total - 1).astype(F32) * (1.0 / total)
    shift = lax.shift_right_arithmetic(scaled(row * size), bits) - row * size
    leading = lax.shift_right_arithmetic(place, bits) - (row * size + lane) == shift
    rest = 1.0 - weight

    def rows_up(values):
        moved = pltpu.roll(values, size - 1, 0)
        return jnp.where(row == size - 1, 0.0, moved)

    def rows_down(values):
        moved = pltpu.roll(values, 1, 0)
        return jnp.where(row == 0, 0.0, moved)

    def lanes(values, index):
        return jnp.take_along_axis(values, jnp.bitwise_and(index, size - 1), axis=1, mode="promise_in_bounds")

    def sample(values):
        below, above = rows_down(values), rows_up(values)

        def displaced(by):
            source = jnp.where(lane < by, above, jnp.where(lane >= by + size, below, values))
            return lanes(source, lane + by)

        centre = displaced(shift)
        return jnp.where(
            leading,
            rest * centre + weight * displaced(shift + 1),
            rest * displaced(shift - 1) + weight * centre,
        )

    def spread(values):
        near, far = rest * values, weight * values
        stay = up = down = 0.0
        for by, part in (
            (shift, jnp.where(leading, near, far)),
            (shift - 1, jnp.where(leading, 0.0, near)),
            (shift + 1, jnp.where(leading, far, 0.0)),
        ):
            moved = lanes(part, lane - by)
            to_next = lane < by
            to_last = lane >= by + size
            down += jnp.where(to_next, moved, 0.0)
            up += jnp.where(to_last, moved, 0.0)
            stay += jnp.where(jnp.logical_or(to_next, to_last), 0.0, moved)
        return stay + rows_down(down) + rows_up(up)

    block = (high_ref[...], low_ref[...])
    block_t = (high_t_ref[...], low_t_ref[...])
    twiddle = (twiddle_ref[0], twiddle_ref[1])
    kernel = (phase_ref[0], phase_ref[1])
    sampled = (sample(field_ref[:, :size]), sample(field_ref[:, size : 2 * size]))
    wave = propagate(sampled, block, block_t, twiddle, kernel, size)
    power = wave[0] * wave[0] + wave[1] * wave[1]
    kept = 1.0 - jnp.sqrt(field_ref[:, 2 * size :] / jnp.maximum(power, 0.01))
    residual = (kept * wave[0], kept * wave[1])
    back = propagate(residual, block, block_t, twiddle, conj(kernel), size)
    out_ref[:, :size] = spread(back[0])
    out_ref[:, size:] = spread(back[1])


def fresnel_phase(fresnel_now, size):
    total = size * size
    period = 64 * total
    index = jnp.arange(size, dtype=jnp.int32)
    frequency = index[:, None] + size * index[None, :]
    signed = jnp.where(frequency < total // 2, frequency, frequency - total)
    turns = fresnel_now * (signed * signed % period) % period
    theta = 2.0 * math.pi / period * turns.astype(F32)
    return jnp.stack([jnp.cos(theta), -jnp.sin(theta)]) * (1.0 / total)


def run_column(scalars, field, phase, size, **options):
    high, low, twiddle = constant_tables(size)
    vmem = pl.BlockSpec(memory_space=pltpu.VMEM)
    return pl.pallas_call(
        partial(column_kernel, size),
        out_shape=jax.ShapeDtypeStruct((size, 2 * size), F32),
        in_specs=[pl.BlockSpec(memory_space=pltpu.SMEM)] + [vmem] * 7,
        out_specs=vmem,
        compiler_params=pltpu.CompilerParams(vmem_limit_bytes=32 * 1024 * 1024),
        name="column",
        **options,
    )(
        scalars,
        field,
        phase,
        jnp.asarray(high),
        jnp.asarray(low),
        jnp.asarray(high.T),
        jnp.asarray(low.T),
        jnp.asarray(twiddle),
    )


def body(object_re, object_im, intensity, shrink, offset, fresnel):
    size = object_re.shape[0]
    tile_count = lax.axis_size("tile")
    phase = fresnel_phase(fresnel[0], size)
    columns = jnp.concatenate([object_re.T, object_im.T, intensity[0].T], axis=1)
    columns = columns.reshape(tile_count, 1, 3 * size)
    field = lax.all_to_all(columns, "tile", split_axis=0, concat_axis=0, tiled=True)
    field = field.reshape(tile_count, 3 * size)
    gradient = run_column(jnp.concatenate([shrink, offset]), field, phase, size)
    tiles = lax.all_to_all(
        gradient.reshape(tile_count, 1, 2 * size), "tile", split_axis=0, concat_axis=0, tiled=True
    ).reshape(tile_count, 2 * size)
    total = tiles.T
    for partner in (1, 2):
        pairs = [(i, i ^ partner) for i in range(lax.axis_size("dist"))]
        total = total + lax.ppermute(total, "dist", pairs)
    return (total[:size], total[size:])


def solution(mesh):
    in_specs = (
        P("tile", None),
        P("tile", None),
        P("dist", "tile", None),
        P("dist"),
        P("dist"),
        P("dist"),
    )
    out_specs = (P("tile", None), P("tile", None))
    return jax.shard_map(body, mesh=mesh, in_specs=in_specs, out_specs=out_specs, check_vma=False)
```

```python
from functools import partial
import math

import jax
import jax.numpy as jnp
import numpy as np
from jax import lax
from jax.experimental import pallas as pl
from jax.experimental.pallas import tpu as pltpu
from jax.sharding import PartitionSpec as P

F32 = jnp.float32
BF16 = jnp.bfloat16


def two_terms(values):
    high = values.astype(BF16)
    low = (values - high.astype(np.float32)).astype(BF16)
    return high, low


def constant_tables(size):
    index = np.arange(size, dtype=np.int64)
    product = np.outer(index, index)
    angle = 2.0 * np.pi / size * (product % size)
    real, imag = np.cos(angle), -np.sin(angle)
    block = np.block([[real, -imag], [imag, real]]).astype(np.float32)
    angle = 2.0 * np.pi / (size * size) * product
    twiddle = np.stack([np.cos(angle), -np.sin(angle)]).astype(np.float32)
    return two_terms(block) + (twiddle,)


def split(values):
    high = values.astype(BF16)
    return high, (values - high.astype(F32)).astype(BF16)


def product(left, right):
    dot = partial(jnp.dot, preferred_element_type=F32)
    return dot(left[0], right[0]) + (dot(left[0], right[1]) + dot(left[1], right[0]))


def times(first, second):
    return (
        first[0] * second[0] - first[1] * second[1],
        first[0] * second[1] + first[1] * second[0],
    )


def conj(pair):
    return (pair[0], -pair[1])


def propagate(values, block, block_t, twiddle, kernel, size):
    def by_rows(table, pair):
        out = product(table, split(jnp.concatenate(pair, axis=0)))
        return (out[:size], out[size:])

    def by_lanes(pair, table):
        out = product(split(jnp.concatenate(pair, axis=1)), table)
        return (out[:, :size], out[:, size:])

    mixed = times(by_rows(block, values), twiddle)
    spectrum = times(by_lanes(mixed, block_t), kernel)
    mixed = times(by_lanes(spectrum, block), conj(twiddle))
    return by_rows(block_t, mixed)


def column_kernel(size, scalars, field_ref, phase_ref, high_ref, low_ref, high_t_ref, low_t_ref, twiddle_ref, out_ref):
    shape = (size, size)
    row = lax.broadcasted_iota(jnp.int32, shape, 0)
    lane = lax.broadcasted_iota(jnp.int32, shape, 1)
    total = size * size
    bits = total.bit_length() - 1
    shrink, offset = scalars[0], scalars[1]

    def scaled(index):
        centre = total // 2
        return centre * total + (index - centre) * (total - shrink) + offset * total

    place = scaled(row * size + lane)
    weight = jnp.bitwise_and(place, total - 1).astype(F32) * (1.0 / total)
    shift = lax.shift_right_arithmetic(scaled(row * size), bits) - row * size
    leading = lax.shift_right_arithmetic(place, bits) - (row * size + lane) == shift
    rest = 1.0 - weight

    def rows_up(values):
        moved = pltpu.roll(values, size - 1, 0)
        return jnp.where(row == size - 1, 0.0, moved)

    def rows_down(values):
        moved = pltpu.roll(values, 1, 0)
        return jnp.where(row == 0, 0.0, moved)

    def lanes(values, index):
        return jnp.take_along_axis(values, jnp.bitwise_and(index, size - 1), axis=1, mode="promise_in_bounds")

    def sample(values):
        below, above = rows_down(values), rows_up(values)

        def displaced(by):
            source = jnp.where(lane < by, above, jnp.where(lane >= by + size, below, values))
            return lanes(source, lane + by)

        centre = displaced(shift)
        return jnp.where(
            leading,
            rest * centre + weight * displaced(shift + 1),
            rest * displaced(shift - 1) + weight * centre,
        )

    def spread(values):
        near, far = rest * values, weight * values
        stay = up = down = 0.0
        for by, part in (
            (shift, jnp.where(leading, near, far)),
            (shift - 1, jnp.where(leading, 0.0, near)),
            (shift + 1, jnp.where(leading, far, 0.0)),
        ):
            moved = lanes(part, lane - by)
            to_next = lane < by
            to_last = lane >= by + size
            down += jnp.where(to_next, moved, 0.0)
            up += jnp.where(to_last, moved, 0.0)
            stay += jnp.where(jnp.logical_or(to_next, to_last), 0.0, moved)
        return stay + rows_down(down) + rows_up(up)

    block = (high_ref[...], low_ref[...])
    block_t = (high_t_ref[...], low_t_ref[...])
    twiddle = (twiddle_ref[0], twiddle_ref[1])
    kernel = (phase_ref[0], phase_ref[1])
    object_re, object_im, measured = (field_ref[pl.ds(part, size, stride=3), :] for part in range(3))
    wave = propagate((sample(object_re), sample(object_im)), block, block_t, twiddle, kernel, size)
    power = wave[0] * wave[0] + wave[1] * wave[1]
    kept = 1.0 - jnp.sqrt(measured / jnp.maximum(power, 0.01))
    residual = (kept * wave[0], kept * wave[1])
    back = propagate(residual, block, block_t, twiddle, conj(kernel), size)
    for part in range(2):
        out_ref[pl.ds(part, size, stride=2), :] = spread(back[part])


def fresnel_phase(fresnel_now, size):
    total = size * size
    period = 64 * total
    index = jnp.arange(size, dtype=jnp.int32)
    frequency = index[:, None] + size * index[None, :]
    signed = jnp.where(frequency < total // 2, frequency, frequency - total)
    turns = fresnel_now * (signed * signed % period) % period
    theta = 2.0 * math.pi / period * turns.astype(F32)
    return jnp.stack([jnp.cos(theta), -jnp.sin(theta)]) * (1.0 / total)


def run_column(scalars, field, phase, size, **options):
    high, low, twiddle = constant_tables(size)
    vmem = pl.BlockSpec(memory_space=pltpu.VMEM)
    return pl.pallas_call(
        partial(column_kernel, size),
        out_shape=jax.ShapeDtypeStruct((2 * size, size), F32),
        in_specs=[pl.BlockSpec(memory_space=pltpu.SMEM)] + [vmem] * 7,
        out_specs=vmem,
        compiler_params=pltpu.CompilerParams(vmem_limit_bytes=32 * 1024 * 1024),
        name="column",
        **options,
    )(
        scalars,
        field,
        phase,
        jnp.asarray(high),
        jnp.asarray(low),
        jnp.asarray(high.T),
        jnp.asarray(low.T),
        jnp.asarray(twiddle),
    )


def pack_kernel(size, re_ref, im_ref, intensity_ref, out_ref):
    for part, ref in enumerate((re_ref, im_ref, intensity_ref)):
        out_ref[pl.ds(part, size, stride=3), :] = ref[...].T


def finish_kernel(size, count, tiles_ref, re_ref, im_ref):
    for part, ref in enumerate((re_ref, im_ref)):
        total = tiles_ref[pl.ds(part, size, stride=2), :]
        for other in range(1, count):
            total = total + tiles_ref[pl.ds(2 * size * other + part, size, stride=2), :]
        ref[...] = total.T


def exchange(rows):
    moved = lax.all_to_all(rows[:, None, :], "tile", split_axis=0, concat_axis=0, tiled=True)
    return moved[:, 0, :]


def body(object_re, object_im, intensity, shrink, offset, fresnel):
    size = object_re.shape[0]
    dist_count = lax.axis_size("dist")
    vmem = pl.BlockSpec(memory_space=pltpu.VMEM)
    phase = fresnel_phase(fresnel[0], size)
    columns = pl.pallas_call(
        partial(pack_kernel, size),
        out_shape=jax.ShapeDtypeStruct((3 * size, size), F32),
        in_specs=[vmem] * 3,
        out_specs=vmem,
        name="pack",
    )(object_re, object_im, intensity[0])
    field = exchange(columns)
    gradient = run_column(jnp.concatenate([shrink, offset]), field, phase, size)
    tiles = exchange(gradient)
    tiles = lax.all_gather(tiles, "dist", axis=0, tiled=True)
    out = jax.ShapeDtypeStruct((size, size), F32)
    return pl.pallas_call(
        partial(finish_kernel, size, dist_count),
        out_shape=(out, out),
        in_specs=[vmem],
        out_specs=(vmem, vmem),
        name="finish",
    )(tiles)


def solution(mesh):
    in_specs = (
        P("tile", None),
        P("tile", None),
        P("dist", "tile", None),
        P("dist"),
        P("dist"),
        P("dist"),
    )
    out_specs = (P("tile", None), P("tile", None))
    return jax.shard_map(body, mesh=mesh, in_specs=in_specs, out_specs=out_specs, check_vma=False)
```

```python
from functools import partial
import math

import jax
import jax.numpy as jnp
import numpy as np
from jax import lax
from jax.experimental import pallas as pl
from jax.experimental.pallas import tpu as pltpu
from jax.sharding import PartitionSpec as P

F32 = jnp.float32
BF16 = jnp.bfloat16
LAYERS = 16


def two_terms(values):
    high = values.astype(BF16)
    low = (values - high.astype(np.float32)).astype(BF16)
    return high, low


def tile_order(size):
    inner = size // LAYERS
    bits = LAYERS.bit_length() - 1
    layers = [int(format(layer, f"0{bits}b")[::-1], 2) for layer in range(LAYERS)]
    return layers, [place * LAYERS + layer for layer in layers for place in range(inner)]


def constant_tables(size):
    index = np.arange(size, dtype=np.int64)
    product = np.outer(index, index)
    angle = 2.0 * np.pi / size * (product % size)
    real, imag = np.cos(angle), -np.sin(angle)
    inner = size // LAYERS
    tile = index % inner * LAYERS + index // inner
    tables = []
    for order in (tile, index):
        part, other = real[:, order], imag[:, order]
        block = np.block([[part, -other], [other, part]]).astype(np.float32)
        tables += two_terms(block) + two_terms(block.T)
    angle = 2.0 * np.pi / (size * size) * product
    twiddle = np.stack([np.cos(angle), -np.sin(angle)]).astype(np.float32)
    return np.concatenate(tables), twiddle


def split(values):
    high = values.astype(BF16)
    return high, (values - high.astype(F32)).astype(BF16)


def product(left, right):
    dot = partial(jnp.dot, preferred_element_type=F32)
    return dot(left[0], right[0]) + (dot(left[0], right[1]) + dot(left[1], right[0]))


def times(first, second):
    return (
        first[0] * second[0] - first[1] * second[1],
        first[0] * second[1] + first[1] * second[0],
    )


def conj(pair):
    return (pair[0], -pair[1])


def propagate(values, tables, twiddle, kernel, size):
    rows, rows_t, lanes, lanes_t = tables

    def by_rows(table, pair):
        out = product(table, split(jnp.concatenate(pair, axis=0)))
        return (out[:size], out[size:])

    def by_lanes(pair, table):
        out = product(split(jnp.concatenate(pair, axis=1)), table)
        return (out[:, :size], out[:, size:])

    mixed = times(by_rows(rows, values), twiddle)
    spectrum = times(by_lanes(mixed, lanes_t), kernel)
    mixed = times(by_lanes(spectrum, lanes), conj(twiddle))
    return by_rows(rows_t, mixed)


def column_kernel(size, scalars, field_ref, phase_ref, table_ref, twiddle_ref, out_ref):
    shape = (size, size)
    inner = size // LAYERS
    slots = tile_order(size)[0]
    line = lax.broadcasted_iota(jnp.int32, shape, 0)
    row = line % inner * LAYERS + line // inner
    lane = lax.broadcasted_iota(jnp.int32, shape, 1)
    total = size * size
    bits = total.bit_length() - 1
    shrink, offset = scalars[0], scalars[1]

    def scaled(index):
        centre = total // 2
        return centre * total + (index - centre) * (total - shrink) + offset * total

    position = scaled(row * size + lane)
    weight = jnp.bitwise_and(position, total - 1).astype(F32) * (1.0 / total)
    shift = lax.shift_right_arithmetic(scaled(row * size), bits) - row * size
    leading = lax.shift_right_arithmetic(position, bits) - (row * size + lane) == shift
    rest = 1.0 - weight

    place = lax.broadcasted_iota(jnp.int32, (inner, size), 0)

    def rows_up(values):
        edge = pltpu.roll(values[:inner], inner - 1, 0)
        return jnp.concatenate([values[inner:], jnp.where(place == inner - 1, 0.0, edge)], axis=0)

    def rows_down(values):
        edge = pltpu.roll(values[size - inner :], 1, 0)
        return jnp.concatenate([jnp.where(place == 0, 0.0, edge), values[: size - inner]], axis=0)

    def lanes(values, index):
        return jnp.take_along_axis(values, jnp.bitwise_and(index, size - 1), axis=1, mode="promise_in_bounds")

    def sample(values):
        below, above = rows_down(values), rows_up(values)

        def displaced(by):
            source = jnp.where(lane < by, above, jnp.where(lane >= by + size, below, values))
            return lanes(source, lane + by)

        centre = displaced(shift)
        return jnp.where(
            leading,
            rest * centre + weight * displaced(shift + 1),
            rest * displaced(shift - 1) + weight * centre,
        )

    def spread(values):
        near, far = rest * values, weight * values
        stay = up = down = 0.0
        for by, part in (
            (shift, jnp.where(leading, near, far)),
            (shift - 1, jnp.where(leading, 0.0, near)),
            (shift + 1, jnp.where(leading, far, 0.0)),
        ):
            moved = lanes(part, lane - by)
            to_next = lane < by
            to_last = lane >= by + size
            down += jnp.where(to_next, moved, 0.0)
            up += jnp.where(to_last, moved, 0.0)
            stay += jnp.where(jnp.logical_or(to_next, to_last), 0.0, moved)
        return stay + rows_down(down) + rows_up(up)

    def gathered(part, count):
        pieces = [field_ref[pl.ds(count * inner * slot + part, inner, stride=count), :] for slot in slots]
        return jnp.concatenate(pieces, axis=0)

    span = 2 * size
    terms = [table_ref[pl.ds(span * term, span), :] for term in range(8)]
    tables = [(terms[2 * term], terms[2 * term + 1]) for term in range(4)]
    twiddle = (twiddle_ref[0], twiddle_ref[1])
    kernel = (phase_ref[0], phase_ref[1])
    object_re, object_im, measured = (gathered(part, 3) for part in range(3))
    wave = propagate((sample(object_re), sample(object_im)), tables, twiddle, kernel, size)
    power = wave[0] * wave[0] + wave[1] * wave[1]
    kept = 1.0 - jnp.sqrt(measured / jnp.maximum(power, 0.01))
    residual = (kept * wave[0], kept * wave[1])
    back = propagate(residual, tables, twiddle, conj(kernel), size)
    for part in range(2):
        result = spread(back[part])
        for layer, slot in enumerate(slots):
            out_ref[pl.ds(2 * inner * slot + part, inner, stride=2), :] = result[inner * layer : inner * (layer + 1)]


def fresnel_phase(fresnel_now, size):
    total = size * size
    period = 64 * total
    index = jnp.arange(size, dtype=jnp.int32)
    frequency = index[:, None] + size * index[None, :]
    signed = jnp.where(frequency < total // 2, frequency, frequency - total)
    turns = fresnel_now * (signed * signed % period) % period
    theta = 2.0 * math.pi / period * turns.astype(F32)
    return jnp.stack([jnp.cos(theta), -jnp.sin(theta)]) * (1.0 / total)


def run_column(scalars, field, phase, size, **options):
    tables, twiddle = constant_tables(size)
    vmem = pl.BlockSpec(memory_space=pltpu.VMEM)
    return pl.pallas_call(
        partial(column_kernel, size),
        out_shape=jax.ShapeDtypeStruct((2 * size, size), F32),
        in_specs=[pl.BlockSpec(memory_space=pltpu.SMEM)] + [vmem] * 4,
        out_specs=vmem,
        compiler_params=pltpu.CompilerParams(vmem_limit_bytes=32 * 1024 * 1024),
        name="column",
        **options,
    )(
        scalars,
        field,
        phase,
        jnp.asarray(tables),
        jnp.asarray(twiddle),
    )


def pack_kernel(size, re_ref, im_ref, intensity_ref, out_ref):
    for part, ref in enumerate((re_ref, im_ref, intensity_ref)):
        out_ref[pl.ds(part, size, stride=3), :] = ref[...].T


def finish_kernel(size, count, tiles_ref, re_ref, im_ref):
    for part, ref in enumerate((re_ref, im_ref)):
        total = tiles_ref[pl.ds(part, size, stride=2), :]
        for other in range(1, count):
            total = total + tiles_ref[pl.ds(2 * size * other + part, size, stride=2), :]
        ref[...] = total.T


def exchange(rows):
    groups = [tile_order(lax.axis_size("tile"))[1]]
    moved = lax.all_to_all(rows[:, None, :], "tile", 0, 0, axis_index_groups=groups, tiled=True)
    return moved[:, 0, :]


def body(object_re, object_im, intensity, shrink, offset, fresnel):
    size = object_re.shape[0]
    dist_count = lax.axis_size("dist")
    vmem = pl.BlockSpec(memory_space=pltpu.VMEM)
    phase = fresnel_phase(fresnel[0], size)
    columns = pl.pallas_call(
        partial(pack_kernel, size),
        out_shape=jax.ShapeDtypeStruct((3 * size, size), F32),
        in_specs=[vmem] * 3,
        out_specs=vmem,
        name="pack",
    )(object_re, object_im, intensity[0])
    field = exchange(columns)
    gradient = run_column(jnp.concatenate([shrink, offset]), field, phase, size)
    tiles = exchange(gradient)
    tiles = lax.all_gather(tiles, "dist", axis=0, tiled=True)
    out = jax.ShapeDtypeStruct((size, size), F32)
    return pl.pallas_call(
        partial(finish_kernel, size, dist_count),
        out_shape=(out, out),
        in_specs=[vmem],
        out_specs=(vmem, vmem),
        compiler_params=pltpu.CompilerParams(vmem_limit_bytes=8 * 1024 * 1024),
        name="finish",
    )(tiles)


def solution(mesh):
    in_specs = (
        P("tile", None),
        P("tile", None),
        P("dist", "tile", None),
        P("dist"),
        P("dist"),
        P("dist"),
    )
    out_specs = (P("tile", None), P("tile", None))
    return jax.shard_map(body, mesh=mesh, in_specs=in_specs, out_specs=out_specs, check_vma=False)
```

```python
from functools import partial
import math

import jax
import jax.numpy as jnp
import numpy as np
from jax import lax
from jax.experimental import pallas as pl
from jax.experimental.pallas import tpu as pltpu
from jax.sharding import PartitionSpec as P

F32 = jnp.float32
BF16 = jnp.bfloat16
LAYERS = 16


def two_terms(values):
    high = values.astype(BF16)
    low = (values - high.astype(np.float32)).astype(BF16)
    return high, low


def place_of(index, inner):
    return (index + 3 * inner // 4) % inner


def layer_slots():
    bits = LAYERS.bit_length() - 1
    return [int(format(layer ^ LAYERS // 2, f"0{bits}b")[::-1], 2) for layer in range(LAYERS)]


def tile_order(size):
    inner = size // LAYERS
    layers = sorted(range(LAYERS), key=layer_slots().__getitem__)
    return [place_of(index, inner) * LAYERS + layer for layer in layers for index in range(inner)]


def constant_tables(size):
    index = np.arange(size, dtype=np.int64)
    product = np.outer(index, index)
    angle = 2.0 * np.pi / size * (product % size)
    real, imag = np.cos(angle), -np.sin(angle)
    inner = size // LAYERS
    tile = place_of(index % inner, inner) * LAYERS + index // inner
    tables = []
    for order in (tile, index):
        part, other = real[:, order], imag[:, order]
        block = np.block([[part, -other], [other, part]]).astype(np.float32)
        tables += two_terms(block) + two_terms(block.T)
    angle = 2.0 * np.pi / (size * size) * product
    twiddle = np.stack([np.cos(angle), -np.sin(angle)]).astype(np.float32)
    return np.concatenate(tables), twiddle


def split(values):
    high = values.astype(BF16)
    return high, (values - high.astype(F32)).astype(BF16)


def product(left, right):
    dot = partial(jnp.dot, preferred_element_type=F32)
    return dot(left[0], right[0]) + (dot(left[0], right[1]) + dot(left[1], right[0]))


def times(first, second):
    return (
        first[0] * second[0] - first[1] * second[1],
        first[0] * second[1] + first[1] * second[0],
    )


def conj(pair):
    return (pair[0], -pair[1])


def propagate(values, tables, twiddle, kernel, size):
    rows, rows_t, lanes, lanes_t = tables

    def by_rows(table, pair):
        out = product(table, split(jnp.concatenate(pair, axis=0)))
        return (out[:size], out[size:])

    def by_lanes(pair, table):
        out = product(split(jnp.concatenate(pair, axis=1)), table)
        return (out[:, :size], out[:, size:])

    mixed = times(by_rows(rows, values), twiddle)
    spectrum = times(by_lanes(mixed, lanes_t), kernel)
    mixed = times(by_lanes(spectrum, lanes), conj(twiddle))
    return by_rows(rows_t, mixed)


def column_kernel(size, scalars, field_ref, phase_ref, table_ref, twiddle_ref, out_ref):
    shape = (size, size)
    inner = size // LAYERS
    slots = layer_slots()
    line = lax.broadcasted_iota(jnp.int32, shape, 0)
    row = place_of(line % inner, inner) * LAYERS + line // inner
    lane = lax.broadcasted_iota(jnp.int32, shape, 1)
    total = size * size
    bits = total.bit_length() - 1
    shrink, offset = scalars[0], scalars[1]

    def scaled(index):
        centre = total // 2
        return centre * total + (index - centre) * (total - shrink) + offset * total

    position = scaled(row * size + lane)
    weight = jnp.bitwise_and(position, total - 1).astype(F32) * (1.0 / total)
    shift = lax.shift_right_arithmetic(scaled(row * size), bits) - row * size
    leading = lax.shift_right_arithmetic(position, bits) - (row * size + lane) == shift
    rest = 1.0 - weight

    place = place_of(lax.broadcasted_iota(jnp.int32, (inner, size), 0), inner)

    def rows_up(values):
        edge = pltpu.roll(values[:inner], inner - 1, 0)
        return jnp.concatenate([values[inner:], jnp.where(place == inner - 1, 0.0, edge)], axis=0)

    def rows_down(values):
        edge = pltpu.roll(values[size - inner :], 1, 0)
        return jnp.concatenate([jnp.where(place == 0, 0.0, edge), values[: size - inner]], axis=0)

    def lanes(values, index):
        return jnp.take_along_axis(values, jnp.bitwise_and(index, size - 1), axis=1, mode="promise_in_bounds")

    def sample(values):
        below, above = rows_down(values), rows_up(values)

        def displaced(by):
            source = jnp.where(lane < by, above, jnp.where(lane >= by + size, below, values))
            return lanes(source, lane + by)

        centre = displaced(shift)
        return jnp.where(
            leading,
            rest * centre + weight * displaced(shift + 1),
            rest * displaced(shift - 1) + weight * centre,
        )

    def spread(values):
        near, far = rest * values, weight * values
        stay = up = down = 0.0
        for by, part in (
            (shift, jnp.where(leading, near, far)),
            (shift - 1, jnp.where(leading, 0.0, near)),
            (shift + 1, jnp.where(leading, far, 0.0)),
        ):
            moved = lanes(part, lane - by)
            to_next = lane < by
            to_last = lane >= by + size
            down += jnp.where(to_next, moved, 0.0)
            up += jnp.where(to_last, moved, 0.0)
            stay += jnp.where(jnp.logical_or(to_next, to_last), 0.0, moved)
        return stay + rows_down(down) + rows_up(up)

    def gathered(part, count):
        pieces = [field_ref[pl.ds(count * inner * slot + part, inner, stride=count), :] for slot in slots]
        return jnp.concatenate(pieces, axis=0)

    span = 2 * size
    terms = [table_ref[pl.ds(span * term, span), :] for term in range(8)]
    tables = [(terms[2 * term], terms[2 * term + 1]) for term in range(4)]
    twiddle = (twiddle_ref[0], twiddle_ref[1])
    kernel = (phase_ref[0], phase_ref[1])
    object_re, object_im, measured = (gathered(part, 3) for part in range(3))
    wave = propagate((sample(object_re), sample(object_im)), tables, twiddle, kernel, size)
    power = wave[0] * wave[0] + wave[1] * wave[1]
    kept = 1.0 - jnp.sqrt(measured / jnp.maximum(power, 0.01))
    residual = (kept * wave[0], kept * wave[1])
    back = propagate(residual, tables, twiddle, conj(kernel), size)
    for part in range(2):
        result = spread(back[part])
        for layer, slot in enumerate(slots):
            out_ref[pl.ds(2 * inner * slot + part, inner, stride=2), :] = result[inner * layer : inner * (layer + 1)]


def fresnel_phase(fresnel_now, size):
    total = size * size
    period = 64 * total
    index = jnp.arange(size, dtype=jnp.int32)
    frequency = index[:, None] + size * index[None, :]
    signed = jnp.where(frequency < total // 2, frequency, frequency - total)
    turns = fresnel_now * (signed * signed % period) % period
    theta = 2.0 * math.pi / period * turns.astype(F32)
    return jnp.stack([jnp.cos(theta), -jnp.sin(theta)]) * (1.0 / total)


def run_column(scalars, field, phase, size, **options):
    tables, twiddle = constant_tables(size)
    vmem = pl.BlockSpec(memory_space=pltpu.VMEM)
    return pl.pallas_call(
        partial(column_kernel, size),
        out_shape=jax.ShapeDtypeStruct((2 * size, size), F32),
        in_specs=[pl.BlockSpec(memory_space=pltpu.SMEM)] + [vmem] * 4,
        out_specs=vmem,
        compiler_params=pltpu.CompilerParams(vmem_limit_bytes=32 * 1024 * 1024),
        name="column",
        **options,
    )(
        scalars,
        field,
        phase,
        jnp.asarray(tables),
        jnp.asarray(twiddle),
    )


def pack_kernel(size, re_ref, im_ref, intensity_ref, out_ref):
    for part, ref in enumerate((re_ref, im_ref, intensity_ref)):
        out_ref[pl.ds(part, size, stride=3), :] = ref[...].T


def finish_kernel(size, count, tiles_ref, re_ref, im_ref):
    for part, ref in enumerate((re_ref, im_ref)):
        total = tiles_ref[pl.ds(part, size, stride=2), :]
        for other in range(1, count):
            total = total + tiles_ref[pl.ds(2 * size * other + part, size, stride=2), :]
        ref[...] = total.T


def exchange(rows):
    groups = [tile_order(lax.axis_size("tile"))]
    moved = lax.all_to_all(rows[:, None, :], "tile", 0, 0, axis_index_groups=groups, tiled=True)
    return moved[:, 0, :]


def body(object_re, object_im, intensity, shrink, offset, fresnel):
    size = object_re.shape[0]
    dist_count = lax.axis_size("dist")
    vmem = pl.BlockSpec(memory_space=pltpu.VMEM)
    phase = fresnel_phase(fresnel[0], size)
    columns = pl.pallas_call(
        partial(pack_kernel, size),
        out_shape=jax.ShapeDtypeStruct((3 * size, size), F32),
        in_specs=[vmem] * 3,
        out_specs=vmem,
        name="pack",
    )(object_re, object_im, intensity[0])
    field = exchange(columns)
    gradient = run_column(jnp.concatenate([shrink, offset]), field, phase, size)
    tiles = exchange(gradient)
    tiles = lax.all_gather(tiles, "dist", axis=0, tiled=True)
    out = jax.ShapeDtypeStruct((size, size), F32)
    return pl.pallas_call(
        partial(finish_kernel, size, dist_count),
        out_shape=(out, out),
        in_specs=[vmem],
        out_specs=(vmem, vmem),
        compiler_params=pltpu.CompilerParams(vmem_limit_bytes=8 * 1024 * 1024),
        name="finish",
    )(tiles)


def solution(mesh):
    in_specs = (
        P("tile", None),
        P("tile", None),
        P("dist", "tile", None),
        P("dist"),
        P("dist"),
        P("dist"),
    )
    out_specs = (P("tile", None), P("tile", None))
    return jax.shard_map(body, mesh=mesh, in_specs=in_specs, out_specs=out_specs, check_vma=False)
```

```python
from functools import partial
import math

import jax
import jax.numpy as jnp
import numpy as np
from jax import lax
from jax.experimental import pallas as pl
from jax.experimental.pallas import tpu as pltpu
from jax.sharding import PartitionSpec as P

F32 = jnp.float32
BF16 = jnp.bfloat16
LAYERS = 16


def two_terms(values):
    high = values.astype(BF16)
    low = (values - high.astype(np.float32)).astype(BF16)
    return high, low


def place_of(index, inner):
    return (index + 3 * inner // 4) % inner


def layer_slots():
    bits = LAYERS.bit_length() - 1
    return [int(format(layer ^ LAYERS // 2, f"0{bits}b")[::-1], 2) for layer in range(LAYERS)]


def tile_order(size):
    inner = size // LAYERS
    layers = sorted(range(LAYERS), key=layer_slots().__getitem__)
    return [place_of(index, inner) * LAYERS + layer for layer in layers for index in range(inner)]


def constant_tables(size):
    index = np.arange(size, dtype=np.int64)
    product = np.outer(index, index)
    angle = 2.0 * np.pi / size * (product % size)
    real, imag = np.cos(angle), -np.sin(angle)
    inner = size // LAYERS
    tile = place_of(index % inner, inner) * LAYERS + index // inner
    tables = []
    for order in (tile, index):
        part, other = real[:, order], imag[:, order]
        block = np.block([[part, -other], [other, part]]).astype(np.float32)
        tables += two_terms(block) + two_terms(block.T)
    angle = 2.0 * np.pi / (size * size) * product
    twiddle = np.stack([np.cos(angle), -np.sin(angle)]).astype(np.float32)
    return np.concatenate(tables), twiddle


def split(values):
    high = values.astype(BF16)
    return high, (values - high.astype(F32)).astype(BF16)


def product(left, right):
    dot = partial(jnp.dot, preferred_element_type=F32)
    return dot(left[0], right[0]) + (dot(left[0], right[1]) + dot(left[1], right[0]))


def times(first, second):
    return (
        first[0] * second[0] - first[1] * second[1],
        first[0] * second[1] + first[1] * second[0],
    )


def conj(pair):
    return (pair[0], -pair[1])


def propagate(values, tables, twiddle, kernel, size):
    rows, rows_t, lanes, lanes_t = tables

    def by_rows(table, pair):
        out = product(table, split(jnp.concatenate(pair, axis=0)))
        return (out[:size], out[size:])

    def by_lanes(pair, table):
        out = product(split(jnp.concatenate(pair, axis=1)), table)
        return (out[:, :size], out[:, size:])

    mixed = times(by_rows(rows, values), twiddle)
    spectrum = times(by_lanes(mixed, lanes_t), kernel)
    mixed = times(by_lanes(spectrum, lanes), conj(twiddle))
    return by_rows(rows_t, mixed)


def column_kernel(size, scalars, field_ref, phase_ref, table_ref, twiddle_ref, out_ref):
    shape = (size, size)
    inner = size // LAYERS
    slots = layer_slots()
    line = lax.broadcasted_iota(jnp.int32, shape, 0)
    row = place_of(line % inner, inner) * LAYERS + line // inner
    lane = lax.broadcasted_iota(jnp.int32, shape, 1)
    total = size * size
    bits = total.bit_length() - 1
    shrink, offset = scalars[0], scalars[1]

    def scaled(index):
        centre = total // 2
        return centre * total + (index - centre) * (total - shrink) + offset * total

    position = scaled(row * size + lane)
    weight = jnp.bitwise_and(position, total - 1).astype(F32) * (1.0 / total)
    shift = lax.shift_right_arithmetic(scaled(row * size), bits) - row * size
    leading = lax.shift_right_arithmetic(position, bits) - (row * size + lane) == shift
    rest = 1.0 - weight

    place = place_of(lax.broadcasted_iota(jnp.int32, (inner, size), 0), inner)

    def rows_up(values):
        edge = pltpu.roll(values[:inner], inner - 1, 0)
        return jnp.concatenate([values[inner:], jnp.where(place == inner - 1, 0.0, edge)], axis=0)

    def rows_down(values):
        edge = pltpu.roll(values[size - inner :], 1, 0)
        return jnp.concatenate([jnp.where(place == 0, 0.0, edge), values[: size - inner]], axis=0)

    def lanes(values, index):
        return jnp.take_along_axis(values, jnp.bitwise_and(index, size - 1), axis=1, mode="promise_in_bounds")

    def sample(values):
        below, above = rows_down(values), rows_up(values)

        def displaced(by):
            source = jnp.where(lane < by, above, jnp.where(lane >= by + size, below, values))
            return lanes(source, lane + by)

        centre = displaced(shift)
        return jnp.where(
            leading,
            rest * centre + weight * displaced(shift + 1),
            rest * displaced(shift - 1) + weight * centre,
        )

    def spread(values):
        near, far = rest * values, weight * values
        stay = up = down = 0.0
        for by, part in (
            (shift, jnp.where(leading, near, far)),
            (shift - 1, jnp.where(leading, 0.0, near)),
            (shift + 1, jnp.where(leading, far, 0.0)),
        ):
            moved = lanes(part, lane - by)
            to_next = lane < by
            to_last = lane >= by + size
            down += jnp.where(to_next, moved, 0.0)
            up += jnp.where(to_last, moved, 0.0)
            stay += jnp.where(jnp.logical_or(to_next, to_last), 0.0, moved)
        return stay + rows_down(down) + rows_up(up)

    def gathered(start):
        pieces = [field_ref[pl.ds(start + 2 * inner * slot, inner, stride=2), :] for slot in slots]
        return jnp.concatenate(pieces, axis=0)

    span = 2 * size
    terms = [table_ref[pl.ds(span * term, span), :] for term in range(8)]
    tables = [(terms[2 * term], terms[2 * term + 1]) for term in range(4)]
    twiddle = (twiddle_ref[0], twiddle_ref[1])
    kernel = (phase_ref[0], phase_ref[1])
    measured = jnp.where(core_index() == 0, gathered(1), gathered(span + 1))
    wave = propagate((sample(gathered(0)), sample(gathered(span))), tables, twiddle, kernel, size)
    power = wave[0] * wave[0] + wave[1] * wave[1]
    kept = 1.0 - jnp.sqrt(measured / jnp.maximum(power, 0.01))
    residual = (kept * wave[0], kept * wave[1])
    back = propagate(residual, tables, twiddle, conj(kernel), size)
    for part in range(2):
        result = spread(back[part])
        for layer, slot in enumerate(slots):
            start = size * part + inner * slot
            out_ref[start : start + inner, :] = result[inner * layer : inner * (layer + 1)]


def fresnel_phase(fresnel_now, size):
    total = size * size
    period = 64 * total
    index = jnp.arange(size, dtype=jnp.int32)
    frequency = index[:, None] + size * index[None, :]
    signed = jnp.where(frequency < total // 2, frequency, frequency - total)
    turns = fresnel_now * (signed * signed % period) % period
    theta = 2.0 * math.pi / period * turns.astype(F32)
    return jnp.stack([jnp.cos(theta), -jnp.sin(theta)]) * (1.0 / total)


def run_column(scalars, field, phase, size, **options):
    tables, twiddle = constant_tables(size)
    vmem = pl.BlockSpec(memory_space=pltpu.VMEM)
    return pl.pallas_call(
        partial(column_kernel, size),
        out_shape=jax.ShapeDtypeStruct((2 * size, size), F32),
        in_specs=[pl.BlockSpec(memory_space=pltpu.SMEM)] + [vmem] * 4,
        out_specs=vmem,
        compiler_params=pltpu.CompilerParams(vmem_limit_bytes=16 * 1024 * 1024),
        name="column",
        **options,
    )(
        scalars,
        field,
        phase,
        jnp.asarray(tables),
        jnp.asarray(twiddle),
    )


def core_index():
    return jnp.bitwise_and(lax.axis_index("dist"), 1)


def pack_kernel(size, re_ref, im_ref, intensity_ref, out_ref, tiles, arrived):
    copies = [pltpu.make_async_copy(intensity_ref, tiles.at[1], arrived.at[1])]
    for core, ref in enumerate((re_ref, im_ref)):
        copies.append(pltpu.make_async_copy(ref, tiles.at[0], arrived.at[0]))
        pl.when(core_index() == core)(copies[-1].start)
    copies[0].start()
    copies[1].wait()
    out_ref[pl.ds(0, size, stride=2), :] = tiles[0].T
    copies[0].wait()
    out_ref[pl.ds(1, size, stride=2), :] = tiles[1].T


def finish_kernel(size, tiles_ref, re_ref, im_ref):
    for part, ref in enumerate((re_ref, im_ref)):
        ref[...] = (tiles_ref[pl.ds(size * part, size), :] + tiles_ref[pl.ds(size * (part + 2), size), :]).T


def exchange(rows):
    groups = [tile_order(lax.axis_size("tile"))]
    moved = lax.all_to_all(rows[:, None, :], "tile", 0, 0, axis_index_groups=groups, tiled=True)
    return moved[:, 0, :]


def of_both_cores(rows):
    return lax.all_gather(rows, "dist", axis=0, tiled=True, axis_index_groups=[[0, 1], [2, 3]])


def body(object_re, object_im, intensity, shrink, offset, fresnel):
    size = object_re.shape[0]
    vmem = pl.BlockSpec(memory_space=pltpu.VMEM)
    phase = fresnel_phase(fresnel[0], size)
    columns = pl.pallas_call(
        partial(pack_kernel, size),
        out_shape=jax.ShapeDtypeStruct((2 * size, size), F32),
        in_specs=[pl.BlockSpec(memory_space=pl.ANY)] * 3,
        out_specs=vmem,
        scratch_shapes=[pltpu.VMEM((2, size, size), F32), pltpu.SemaphoreType.DMA((2,))],
        name="pack",
    )(object_re, object_im, intensity[0])
    field = of_both_cores(exchange(columns))
    gradient = run_column(jnp.concatenate([shrink, offset]), field, phase, size)
    first, second = of_both_cores(gradient).reshape(2, 2, size, size)
    own = jnp.where(core_index() == 0, first[0] + second[0], first[1] + second[1])
    tiles = lax.all_gather(exchange(own), "dist", axis=0, tiled=True)
    out = jax.ShapeDtypeStruct((size, size), F32)
    return pl.pallas_call(
        partial(finish_kernel, size),
        out_shape=(out, out),
        in_specs=[vmem],
        out_specs=(vmem, vmem),
        compiler_params=pltpu.CompilerParams(vmem_limit_bytes=8 * 1024 * 1024),
        name="finish",
    )(tiles)


def solution(mesh):
    in_specs = (
        P("tile", None),
        P("tile", None),
        P("dist", "tile", None),
        P("dist"),
        P("dist"),
        P("dist"),
    )
    out_specs = (P("tile", None), P("tile", None))
    return jax.shard_map(body, mesh=mesh, in_specs=in_specs, out_specs=out_specs, check_vma=False)
```

```python
from functools import partial
import math

import jax
import jax.numpy as jnp
import numpy as np
from jax import lax
from jax.experimental import pallas as pl
from jax.experimental.pallas import tpu as pltpu
from jax.sharding import PartitionSpec as P

F32 = jnp.float32
BF16 = jnp.bfloat16
LAYERS = 16


def two_terms(values):
    high = values.astype(BF16)
    low = (values - high.astype(np.float32)).astype(BF16)
    return high, low


def place_of(index, inner):
    return (index + 3 * inner // 4) % inner


def layer_slots():
    bits = LAYERS.bit_length() - 1
    return [int(format(layer ^ LAYERS // 2, f"0{bits}b")[::-1], 2) for layer in range(LAYERS)]


def tile_order(size):
    inner = size // LAYERS
    layers = sorted(range(LAYERS), key=layer_slots().__getitem__)
    return [place_of(index, inner) * LAYERS + layer for layer in layers for index in range(inner)]


def constant_tables(size):
    index = np.arange(size, dtype=np.int64)
    product = np.outer(index, index)
    angle = 2.0 * np.pi / size * (product % size)
    real, imag = np.cos(angle), -np.sin(angle)
    inner = size // LAYERS
    tile = place_of(index % inner, inner) * LAYERS + index // inner
    tables = []
    for order in (tile, index):
        part, other = real[:, order], imag[:, order]
        block = np.block([[part, -other], [other, part]]).astype(np.float32)
        tables += two_terms(block) + two_terms(block.T)
    angle = 2.0 * np.pi / (size * size) * product
    twiddle = np.stack([np.cos(angle), -np.sin(angle)]).astype(np.float32)
    return np.concatenate(tables), twiddle


def split(values):
    high = values.astype(BF16)
    return high, (values - high.astype(F32)).astype(BF16)


def product(left, right):
    dot = partial(jnp.dot, preferred_element_type=F32)
    return dot(left[0], right[0]) + (dot(left[0], right[1]) + dot(left[1], right[0]))


def matmul(left, right):
    return jnp.dot(left, right, preferred_element_type=F32)


def times(first, second):
    return (
        first[0] * second[0] - first[1] * second[1],
        first[0] * second[1] + first[1] * second[0],
    )


def conj(pair):
    return (pair[0], -pair[1])


def propagate(values, tables, twiddle, kernel, size):
    rows, rows_t, lanes, lanes_t = tables

    def by_rows(table, pair):
        high, low = split(jnp.concatenate(pair, axis=0))
        out = matmul(table[0], jnp.concatenate([high, low], axis=1))
        out = out[:, :size] + (out[:, size:] + matmul(table[1], high))
        return (out[:size], out[size:])

    def by_lanes(pair, table):
        high, low = split(jnp.concatenate(pair, axis=1))
        out = matmul(jnp.concatenate([high, low], axis=0), table[0])
        out = out[:size] + (out[size:] + matmul(high, table[1]))
        return (out[:, :size], out[:, size:])

    mixed = times(by_rows(rows, values), twiddle)
    spectrum = times(by_lanes(mixed, lanes_t), kernel)
    mixed = times(by_lanes(spectrum, lanes), conj(twiddle))
    return by_rows(rows_t, mixed)


def column_kernel(size, scalars, field_ref, phase_ref, table_ref, twiddle_ref, out_ref):
    shape = (size, size)
    inner = size // LAYERS
    slots = layer_slots()
    line = lax.broadcasted_iota(jnp.int32, shape, 0)
    row = place_of(line % inner, inner) * LAYERS + line // inner
    lane = lax.broadcasted_iota(jnp.int32, shape, 1)
    total = size * size
    bits = total.bit_length() - 1
    shrink, offset = scalars[0], scalars[1]

    def scaled(index):
        centre = total // 2
        return centre * total + (index - centre) * (total - shrink) + offset * total

    position = scaled(row * size + lane)
    weight = jnp.bitwise_and(position, total - 1).astype(F32) * (1.0 / total)
    shift = lax.shift_right_arithmetic(scaled(row * size), bits) - row * size
    leading = lax.shift_right_arithmetic(position, bits) - (row * size + lane) == shift
    rest = 1.0 - weight

    place = place_of(lax.broadcasted_iota(jnp.int32, (inner, size), 0), inner)

    def rows_up(values):
        edge = pltpu.roll(values[:inner], inner - 1, 0)
        return jnp.concatenate([values[inner:], jnp.where(place == inner - 1, 0.0, edge)], axis=0)

    def rows_down(values):
        edge = pltpu.roll(values[size - inner :], 1, 0)
        return jnp.concatenate([jnp.where(place == 0, 0.0, edge), values[: size - inner]], axis=0)

    def lanes(values, index):
        return jnp.take_along_axis(values, jnp.bitwise_and(index, size - 1), axis=1, mode="promise_in_bounds")

    lower = row * size + lane + jnp.where(leading, shift, shift - 1)

    def sample(values):
        below, above = rows_down(values), rows_up(values)

        def window(first):
            return jnp.where(lane < first, above, jnp.where(lane >= first + size, below, values))

        return rest * lanes(window(shift), lower) + weight * lanes(window(shift + 1), lower + 1)

    def spread(values):
        near, far = rest * values, weight * values
        stay = up = down = 0.0
        for by, part in (
            (shift, jnp.where(leading, near, far)),
            (shift - 1, jnp.where(leading, 0.0, near)),
            (shift + 1, jnp.where(leading, far, 0.0)),
        ):
            moved = lanes(part, lane - by)
            to_next = lane < by
            to_last = lane >= by + size
            down += jnp.where(to_next, moved, 0.0)
            up += jnp.where(to_last, moved, 0.0)
            stay += jnp.where(jnp.logical_or(to_next, to_last), 0.0, moved)
        return stay + rows_down(down) + rows_up(up)

    def gathered(start):
        pieces = [field_ref[pl.ds(start + 2 * inner * slot, inner, stride=2), :] for slot in slots]
        return jnp.concatenate(pieces, axis=0)

    span = 2 * size
    terms = [table_ref[pl.ds(span * term, span), :] for term in range(8)]
    tables = [(terms[2 * term], terms[2 * term + 1]) for term in range(4)]
    twiddle = (twiddle_ref[0], twiddle_ref[1])
    kernel = (phase_ref[0], phase_ref[1])
    measured = jnp.where(core_index() == 0, gathered(1), gathered(span + 1))
    wave = propagate((sample(gathered(0)), sample(gathered(span))), tables, twiddle, kernel, size)
    power = wave[0] * wave[0] + wave[1] * wave[1]
    kept = 1.0 - jnp.sqrt(measured / jnp.maximum(power, 0.01))
    residual = (kept * wave[0], kept * wave[1])
    back = propagate(residual, tables, twiddle, conj(kernel), size)
    for part in range(2):
        result = spread(back[part])
        for layer, slot in enumerate(slots):
            start = size * part + inner * slot
            out_ref[start : start + inner, :] = result[inner * layer : inner * (layer + 1)]


def fresnel_phase(fresnel_now, size):
    total = size * size
    period = 64 * total
    index = jnp.arange(size, dtype=jnp.int32)
    frequency = index[:, None] + size * index[None, :]
    signed = jnp.where(frequency < total // 2, frequency, frequency - total)
    turns = fresnel_now * (signed * signed % period) % period
    theta = 2.0 * math.pi / period * turns.astype(F32)
    return jnp.stack([jnp.cos(theta), -jnp.sin(theta)]) * (1.0 / total)


def run_column(scalars, field, phase, size, **options):
    tables, twiddle = constant_tables(size)
    vmem = pl.BlockSpec(memory_space=pltpu.VMEM)
    return pl.pallas_call(
        partial(column_kernel, size),
        out_shape=jax.ShapeDtypeStruct((2 * size, size), F32),
        in_specs=[pl.BlockSpec(memory_space=pltpu.SMEM)] + [vmem] * 4,
        out_specs=vmem,
        compiler_params=pltpu.CompilerParams(vmem_limit_bytes=16 * 1024 * 1024),
        name="column",
        **options,
    )(
        scalars,
        field,
        phase,
        jnp.asarray(tables),
        jnp.asarray(twiddle),
    )


def core_index():
    return jnp.bitwise_and(lax.axis_index("dist"), 1)


def pack_kernel(size, re_ref, im_ref, intensity_ref, out_ref, tiles, arrived):
    copies = [pltpu.make_async_copy(intensity_ref, tiles.at[1], arrived.at[1])]
    for core, ref in enumerate((re_ref, im_ref)):
        copies.append(pltpu.make_async_copy(ref, tiles.at[0], arrived.at[0]))
        pl.when(core_index() == core)(copies[-1].start)
    copies[0].start()
    copies[1].wait()
    out_ref[pl.ds(0, size, stride=2), :] = tiles[0].T
    copies[0].wait()
    out_ref[pl.ds(1, size, stride=2), :] = tiles[1].T


def finish_kernel(size, tiles_ref, re_ref, im_ref):
    for part, ref in enumerate((re_ref, im_ref)):
        ref[...] = (tiles_ref[pl.ds(size * part, size), :] + tiles_ref[pl.ds(size * (part + 2), size), :]).T


def exchange(rows):
    groups = [tile_order(lax.axis_size("tile"))]
    moved = lax.all_to_all(rows[:, None, :], "tile", 0, 0, axis_index_groups=groups, tiled=True)
    return moved[:, 0, :]


def of_both_cores(rows):
    return lax.all_gather(rows, "dist", axis=0, tiled=True, axis_index_groups=[[0, 1], [2, 3]])


def body(object_re, object_im, intensity, shrink, offset, fresnel):
    size = object_re.shape[0]
    vmem = pl.BlockSpec(memory_space=pltpu.VMEM)
    phase = fresnel_phase(fresnel[0], size)
    columns = pl.pallas_call(
        partial(pack_kernel, size),
        out_shape=jax.ShapeDtypeStruct((2 * size, size), F32),
        in_specs=[pl.BlockSpec(memory_space=pl.ANY)] * 3,
        out_specs=vmem,
        scratch_shapes=[pltpu.VMEM((2, size, size), F32), pltpu.SemaphoreType.DMA((2,))],
        name="pack",
    )(object_re, object_im, intensity[0])
    field = of_both_cores(exchange(columns))
    gradient = run_column(jnp.concatenate([shrink, offset]), field, phase, size)
    first, second = of_both_cores(gradient).reshape(2, 2, size, size)
    own = jnp.where(core_index() == 0, first[0] + second[0], first[1] + second[1])
    tiles = lax.all_gather(exchange(own), "dist", axis=0, tiled=True)
    out = jax.ShapeDtypeStruct((size, size), F32)
    return pl.pallas_call(
        partial(finish_kernel, size),
        out_shape=(out, out),
        in_specs=[vmem],
        out_specs=(vmem, vmem),
        compiler_params=pltpu.CompilerParams(vmem_limit_bytes=8 * 1024 * 1024),
        name="finish",
    )(tiles)


def solution(mesh):
    in_specs = (
        P("tile", None),
        P("tile", None),
        P("dist", "tile", None),
        P("dist"),
        P("dist"),
        P("dist"),
    )
    out_specs = (P("tile", None), P("tile", None))
    return jax.shard_map(body, mesh=mesh, in_specs=in_specs, out_specs=out_specs, check_vma=False)
```

```python
from functools import partial
import math

import jax
import jax.numpy as jnp
import numpy as np
from jax import lax
from jax.experimental import pallas as pl
from jax.experimental.pallas import tpu as pltpu
from jax.sharding import PartitionSpec as P

F32 = jnp.float32
BF16 = jnp.bfloat16
LAYERS = 16


def two_terms(values):
    high = values.astype(BF16)
    low = (values - high.astype(np.float32)).astype(BF16)
    return high, low


def place_of(index, inner):
    return (index + 3 * inner // 4) % inner


def layer_slots():
    bits = LAYERS.bit_length() - 1
    return [int(format(layer ^ LAYERS // 2 + 1, f"0{bits}b")[::-1], 2) for layer in range(LAYERS)]


def tile_order(size):
    inner = size // LAYERS
    layers = sorted(range(LAYERS), key=layer_slots().__getitem__)
    return [place_of(index, inner) * LAYERS + layer for layer in layers for index in range(inner)]


def constant_tables(size):
    index = np.arange(size, dtype=np.int64)
    product = np.outer(index, index)
    angle = 2.0 * np.pi / size * (product % size)
    real, imag = np.cos(angle), -np.sin(angle)
    inner = size // LAYERS
    tile = place_of(index % inner, inner) * LAYERS + index // inner
    tables = []
    for order in (tile, index):
        part, other = real[:, order], imag[:, order]
        block = np.block([[part, -other], [other, part]]).astype(np.float32)
        tables += two_terms(block) + two_terms(block.T)
    angle = 2.0 * np.pi / (size * size) * product
    twiddle = np.stack([np.cos(angle), -np.sin(angle)]).astype(np.float32)
    return np.concatenate(tables), twiddle


def split(values):
    high = values.astype(BF16)
    return high, (values - high.astype(F32)).astype(BF16)


def product(left, right):
    dot = partial(jnp.dot, preferred_element_type=F32)
    return dot(left[0], right[0]) + (dot(left[0], right[1]) + dot(left[1], right[0]))


def matmul(left, right):
    return jnp.dot(left, right, preferred_element_type=F32)


def times(first, second):
    return (
        first[0] * second[0] - first[1] * second[1],
        first[0] * second[1] + first[1] * second[0],
    )


def conj(pair):
    return (pair[0], -pair[1])


def propagate(values, tables, twiddle, kernel, size):
    rows, rows_t, lanes, lanes_t = tables

    def by_rows(table, pair):
        high, low = split(jnp.concatenate(pair, axis=0))
        out = matmul(table[0], jnp.concatenate([high, low], axis=1))
        out = out[:, :size] + (out[:, size:] + matmul(table[1], high))
        return (out[:size], out[size:])

    def by_lanes(pair, table):
        high, low = split(jnp.concatenate(pair, axis=1))
        out = matmul(jnp.concatenate([high, low], axis=0), table[0])
        out = out[:size] + (out[size:] + matmul(high, table[1]))
        return (out[:, :size], out[:, size:])

    mixed = times(by_rows(rows, values), twiddle)
    spectrum = times(by_lanes(mixed, lanes_t), kernel)
    mixed = times(by_lanes(spectrum, lanes), conj(twiddle))
    return by_rows(rows_t, mixed)


def column_kernel(size, scalars, field_ref, phase_ref, table_ref, twiddle_ref, out_ref):
    shape = (size, size)
    inner = size // LAYERS
    slots = layer_slots()
    line = lax.broadcasted_iota(jnp.int32, shape, 0)
    row = place_of(line % inner, inner) * LAYERS + line // inner
    lane = lax.broadcasted_iota(jnp.int32, shape, 1)
    total = size * size
    bits = total.bit_length() - 1
    shrink, offset = scalars[0], scalars[1]

    def scaled(index):
        centre = total // 2
        return centre * total + (index - centre) * (total - shrink) + offset * total

    position = scaled(row * size + lane)
    weight = jnp.bitwise_and(position, total - 1).astype(F32) * (1.0 / total)
    shift = lax.shift_right_arithmetic(scaled(row * size), bits) - row * size
    leading = lax.shift_right_arithmetic(position, bits) - (row * size + lane) == shift
    rest = 1.0 - weight

    place = place_of(lax.broadcasted_iota(jnp.int32, (inner, size), 0), inner)

    def rows_up(values):
        edge = pltpu.roll(values[:inner], inner - 1, 0)
        return jnp.concatenate([values[inner:], jnp.where(place == inner - 1, 0.0, edge)], axis=0)

    def rows_down(values):
        edge = pltpu.roll(values[size - inner :], 1, 0)
        return jnp.concatenate([jnp.where(place == 0, 0.0, edge), values[: size - inner]], axis=0)

    def lanes(values, index):
        return jnp.take_along_axis(values, jnp.bitwise_and(index, size - 1), axis=1, mode="promise_in_bounds")

    lower = row * size + lane + jnp.where(leading, shift, shift - 1)

    def sample(values):
        below, above = rows_down(values), rows_up(values)

        def window(first):
            return jnp.where(lane < first, above, jnp.where(lane >= first + size, below, values))

        return rest * lanes(window(shift), lower) + weight * lanes(window(shift + 1), lower + 1)

    def spread(values):
        near, far = rest * values, weight * values
        stay = up = down = 0.0
        for by, part in (
            (shift, jnp.where(leading, near, far)),
            (shift - 1, jnp.where(leading, 0.0, near)),
            (shift + 1, jnp.where(leading, far, 0.0)),
        ):
            moved = lanes(part, lane - by)
            to_next = lane < by
            to_last = lane >= by + size
            down += jnp.where(to_next, moved, 0.0)
            up += jnp.where(to_last, moved, 0.0)
            stay += jnp.where(jnp.logical_or(to_next, to_last), 0.0, moved)
        return stay + rows_down(down) + rows_up(up)

    def gathered(start):
        pieces = [field_ref[pl.ds(start + 2 * inner * slot, inner, stride=2), :] for slot in slots]
        return jnp.concatenate(pieces, axis=0)

    span = 2 * size
    terms = [table_ref[pl.ds(span * term, span), :] for term in range(8)]
    tables = [(terms[2 * term], terms[2 * term + 1]) for term in range(4)]
    twiddle = (twiddle_ref[0], twiddle_ref[1])
    kernel = (phase_ref[0], phase_ref[1])
    measured = jnp.where(core_index() == 0, gathered(1), gathered(span + 1))
    wave = propagate((sample(gathered(0)), sample(gathered(span))), tables, twiddle, kernel, size)
    power = wave[0] * wave[0] + wave[1] * wave[1]
    kept = 1.0 - jnp.sqrt(measured) * lax.rsqrt(jnp.maximum(power, 0.01))
    residual = (kept * wave[0], kept * wave[1])
    back = propagate(residual, tables, twiddle, conj(kernel), size)
    for part in range(2):
        result = spread(back[part])
        for layer, slot in enumerate(slots):
            start = size * part + inner * slot
            out_ref[start : start + inner, :] = result[inner * layer : inner * (layer + 1)]


def fresnel_phase(fresnel_now, size):
    total = size * size
    period = 64 * total
    index = jnp.arange(size, dtype=jnp.int32)
    frequency = index[:, None] + size * index[None, :]
    signed = jnp.where(frequency < total // 2, frequency, frequency - total)
    turns = fresnel_now * (signed * signed % period) % period
    theta = 2.0 * math.pi / period * turns.astype(F32)
    return jnp.stack([jnp.cos(theta), -jnp.sin(theta)]) * (1.0 / total)


def run_column(scalars, field, phase, size, **options):
    tables, twiddle = constant_tables(size)
    vmem = pl.BlockSpec(memory_space=pltpu.VMEM)
    return pl.pallas_call(
        partial(column_kernel, size),
        out_shape=jax.ShapeDtypeStruct((2 * size, size), F32),
        in_specs=[pl.BlockSpec(memory_space=pltpu.SMEM)] + [vmem] * 4,
        out_specs=vmem,
        compiler_params=pltpu.CompilerParams(vmem_limit_bytes=16 * 1024 * 1024),
        name="column",
        **options,
    )(
        scalars,
        field,
        phase,
        jnp.asarray(tables),
        jnp.asarray(twiddle),
    )


def core_index():
    return jnp.bitwise_and(lax.axis_index("dist"), 1)


def pack_kernel(size, re_ref, im_ref, intensity_ref, out_ref, tiles, arrived):
    copies = [pltpu.make_async_copy(intensity_ref, tiles.at[1], arrived.at[1])]
    for core, ref in enumerate((re_ref, im_ref)):
        copies.append(pltpu.make_async_copy(ref, tiles.at[0], arrived.at[0]))
        pl.when(core_index() == core)(copies[-1].start)
    copies[0].start()
    copies[1].wait()
    out_ref[pl.ds(0, size, stride=2), :] = tiles[0].T
    copies[0].wait()
    out_ref[pl.ds(1, size, stride=2), :] = tiles[1].T


def finish_kernel(size, tiles_ref, re_ref, im_ref):
    for part, ref in enumerate((re_ref, im_ref)):
        ref[...] = (tiles_ref[pl.ds(size * part, size), :] + tiles_ref[pl.ds(size * (part + 2), size), :]).T


def exchange(rows):
    groups = [tile_order(lax.axis_size("tile"))]
    moved = lax.all_to_all(rows[:, None, :], "tile", 0, 0, axis_index_groups=groups, tiled=True)
    return moved[:, 0, :]


def of_both_cores(rows):
    return lax.all_gather(rows, "dist", axis=0, tiled=True, axis_index_groups=[[0, 1], [2, 3]])


def body(object_re, object_im, intensity, shrink, offset, fresnel):
    size = object_re.shape[0]
    vmem = pl.BlockSpec(memory_space=pltpu.VMEM)
    phase = fresnel_phase(fresnel[0], size)
    columns = pl.pallas_call(
        partial(pack_kernel, size),
        out_shape=jax.ShapeDtypeStruct((2 * size, size), F32),
        in_specs=[pl.BlockSpec(memory_space=pl.ANY)] * 3,
        out_specs=vmem,
        scratch_shapes=[pltpu.VMEM((2, size, size), F32), pltpu.SemaphoreType.DMA((2,))],
        name="pack",
    )(object_re, object_im, intensity[0])
    field = of_both_cores(exchange(columns))
    gradient = run_column(jnp.concatenate([shrink, offset]), field, phase, size)
    first, second = of_both_cores(gradient).reshape(2, 2, size, size)
    own = jnp.where(core_index() == 0, first[0] + second[0], first[1] + second[1])
    tiles = lax.all_gather(exchange(own), "dist", axis=0, tiled=True)
    out = jax.ShapeDtypeStruct((size, size), F32)
    return pl.pallas_call(
        partial(finish_kernel, size),
        out_shape=(out, out),
        in_specs=[vmem],
        out_specs=(vmem, vmem),
        compiler_params=pltpu.CompilerParams(vmem_limit_bytes=8 * 1024 * 1024),
        name="finish",
    )(tiles)


def solution(mesh):
    in_specs = (
        P("tile", None),
        P("tile", None),
        P("dist", "tile", None),
        P("dist"),
        P("dist"),
        P("dist"),
    )
    out_specs = (P("tile", None), P("tile", None))
    return jax.shard_map(body, mesh=mesh, in_specs=in_specs, out_specs=out_specs, check_vma=False)
```

```python
from functools import partial
import math

import jax
import jax.numpy as jnp
import numpy as np
from jax import lax
from jax.experimental import pallas as pl
from jax.experimental.pallas import tpu as pltpu
from jax.sharding import PartitionSpec as P

F32 = jnp.float32
BF16 = jnp.bfloat16
LAYERS = 16


def two_terms(values):
    high = values.astype(BF16)
    low = (values - high.astype(np.float32)).astype(BF16)
    return high, low


def place_of(index, inner):
    return (index + 3 * inner // 4) % inner


def layer_slots():
    bits = LAYERS.bit_length() - 1
    return [int(format(layer ^ LAYERS // 2 + 1, f"0{bits}b")[::-1], 2) for layer in range(LAYERS)]


def tile_order(size):
    inner = size // LAYERS
    layers = sorted(range(LAYERS), key=layer_slots().__getitem__)
    return [place_of(index, inner) * LAYERS + layer for layer in layers for index in range(inner)]


def constant_tables(size):
    index = np.arange(size, dtype=np.int64)
    product = np.outer(index, index)
    angle = 2.0 * np.pi / size * (product % size)
    real, imag = np.cos(angle), -np.sin(angle)
    inner = size // LAYERS
    tile = place_of(index % inner, inner) * LAYERS + index // inner
    tables = []
    for order in (tile, index):
        part, other = real[:, order], imag[:, order]
        block = np.block([[part, -other], [other, part]]).astype(np.float32)
        tables += two_terms(block) + two_terms(block.T)
    angle = 2.0 * np.pi / (size * size) * product
    twiddle = np.stack([np.cos(angle), -np.sin(angle)]).astype(np.float32)
    return np.concatenate(tables), twiddle


def split(values):
    high = values.astype(BF16)
    return high, (values - high.astype(F32)).astype(BF16)


def product(left, right):
    dot = partial(jnp.dot, preferred_element_type=F32)
    return dot(left[0], right[0]) + (dot(left[0], right[1]) + dot(left[1], right[0]))


def matmul(left, right):
    return jnp.dot(left, right, preferred_element_type=F32)


def times(first, second):
    return (
        first[0] * second[0] - first[1] * second[1],
        first[0] * second[1] + first[1] * second[0],
    )


def conj(pair):
    return (pair[0], -pair[1])


def propagate(values, tables, twiddle, kernel, size):
    rows, rows_t, lanes, lanes_t = tables

    def by_rows(table, pair):
        high, low = split(jnp.concatenate(pair, axis=0))
        out = matmul(table[0], jnp.concatenate([high, low], axis=1))
        out = out[:, :size] + (out[:, size:] + matmul(table[1], high))
        return (out[:size], out[size:])

    def by_lanes(pair, table):
        high, low = split(jnp.concatenate(pair, axis=1))
        out = matmul(jnp.concatenate([high, low], axis=0), table[0])
        out = out[:size] + (out[size:] + matmul(high, table[1]))
        return (out[:, :size], out[:, size:])

    mixed = times(by_rows(rows, values), twiddle)
    spectrum = times(by_lanes(mixed, lanes_t), kernel)
    mixed = times(by_lanes(spectrum, lanes), conj(twiddle))
    return by_rows(rows_t, mixed)


def column_kernel(size, scalars, field_ref, phase_ref, table_ref, twiddle_ref, out_ref):
    shape = (size, size)
    inner = size // LAYERS
    slots = layer_slots()
    line = lax.broadcasted_iota(jnp.int32, shape, 0)
    row = place_of(line % inner, inner) * LAYERS + line // inner
    lane = lax.broadcasted_iota(jnp.int32, shape, 1)
    total = size * size
    bits = total.bit_length() - 1
    shrink, offset = scalars[0], scalars[1]

    def scaled(index):
        centre = total // 2
        return centre * total + (index - centre) * (total - shrink) + offset * total

    position = scaled(row * size + lane)
    weight = jnp.bitwise_and(position, total - 1).astype(F32) * (1.0 / total)
    shift = lax.shift_right_arithmetic(scaled(row * size), bits) - row * size
    leading = lax.shift_right_arithmetic(position, bits) - (row * size + lane) == shift
    rest = 1.0 - weight

    place = place_of(lax.broadcasted_iota(jnp.int32, (inner, size), 0), inner)

    def rows_up(values):
        edge = pltpu.roll(values[:inner], inner - 1, 0)
        return jnp.concatenate([values[inner:], jnp.where(place == inner - 1, 0.0, edge)], axis=0)

    def rows_down(values):
        edge = pltpu.roll(values[size - inner :], 1, 0)
        return jnp.concatenate([jnp.where(place == 0, 0.0, edge), values[: size - inner]], axis=0)

    def lanes(values, index):
        return jnp.take_along_axis(values, jnp.bitwise_and(index, size - 1), axis=1, mode="promise_in_bounds")

    lower = row * size + lane + jnp.where(leading, shift, shift - 1)

    def sample(values):
        below, above = rows_down(values), rows_up(values)

        def window(first):
            return jnp.where(lane < first, above, jnp.where(lane >= first + size, below, values))

        return rest * lanes(window(shift), lower) + weight * lanes(window(shift + 1), lower + 1)

    def spread(values):
        near, far = rest * values, weight * values
        stay = up = down = 0.0
        for by, part in (
            (shift, jnp.where(leading, near, far)),
            (shift - 1, jnp.where(leading, 0.0, near)),
            (shift + 1, jnp.where(leading, far, 0.0)),
        ):
            moved = lanes(part, lane - by)
            to_next = lane < by
            to_last = lane >= by + size
            down += jnp.where(to_next, moved, 0.0)
            up += jnp.where(to_last, moved, 0.0)
            stay += jnp.where(jnp.logical_or(to_next, to_last), 0.0, moved)
        return stay + rows_down(down) + rows_up(up)

    def gathered(start):
        pieces = [field_ref[pl.ds(start + 2 * inner * slot, inner, stride=2), :] for slot in slots]
        return jnp.concatenate(pieces, axis=0)

    span = 2 * size
    terms = [table_ref[pl.ds(span * term, span), :] for term in range(8)]
    tables = [(terms[2 * term], terms[2 * term + 1]) for term in range(4)]
    twiddle = (twiddle_ref[0], twiddle_ref[1])
    kernel = (phase_ref[0], phase_ref[1])
    measured = jnp.where(core_index() == 0, gathered(1), gathered(span + 1))
    wave = propagate((sample(gathered(0)), sample(gathered(span))), tables, twiddle, kernel, size)
    power = wave[0] * wave[0] + wave[1] * wave[1]
    kept = 1.0 - jnp.sqrt(measured) * lax.rsqrt(jnp.maximum(power, 0.01))
    residual = (kept * wave[0], kept * wave[1])
    back = propagate(residual, tables, twiddle, conj(kernel), size)
    for part in range(2):
        result = spread(back[part])
        for layer, slot in enumerate(slots):
            start = size * part + inner * slot
            out_ref[start : start + inner, :] = result[inner * layer : inner * (layer + 1)]


def fresnel_phase(fresnel_now, size):
    total = size * size
    period = 64 * total
    index = jnp.arange(size, dtype=jnp.int32)
    frequency = index[:, None] + size * index[None, :]
    signed = jnp.where(frequency < total // 2, frequency, frequency - total)
    turns = fresnel_now * (signed * signed % period) % period
    theta = 2.0 * math.pi / period * turns.astype(F32)
    return jnp.stack([jnp.cos(theta), -jnp.sin(theta)]) * (1.0 / total)


def run_column(scalars, field, phase, size, **options):
    tables, twiddle = constant_tables(size)
    vmem = pl.BlockSpec(memory_space=pltpu.VMEM)
    return pl.pallas_call(
        partial(column_kernel, size),
        out_shape=jax.ShapeDtypeStruct((2 * size, size), F32),
        in_specs=[pl.BlockSpec(memory_space=pltpu.SMEM)] + [vmem] * 4,
        out_specs=vmem,
        compiler_params=pltpu.CompilerParams(vmem_limit_bytes=16 * 1024 * 1024),
        name="column",
        **options,
    )(
        scalars,
        field,
        phase,
        jnp.asarray(tables),
        jnp.asarray(twiddle),
    )


def core_index():
    return jnp.bitwise_and(lax.axis_index("dist"), 1)


def pack_kernel(size, re_ref, im_ref, intensity_ref, out_ref, tiles, arrived):
    copies = [pltpu.make_async_copy(intensity_ref, tiles.at[1], arrived.at[1])]
    for core, ref in enumerate((re_ref, im_ref)):
        copies.append(pltpu.make_async_copy(ref, tiles.at[0], arrived.at[0]))
        pl.when(core_index() == core)(copies[-1].start)
    copies[0].start()
    copies[1].wait()
    out_ref[pl.ds(0, size, stride=2), :] = tiles[0].T
    copies[0].wait()
    out_ref[pl.ds(1, size, stride=2), :] = tiles[1].T


def finish_kernel(size, tiles_ref, re_ref, im_ref, parts, sent):
    copies = [pltpu.make_async_copy(parts.at[part], ref, sent.at[part]) for part, ref in enumerate((re_ref, im_ref))]
    for part, copy in enumerate(copies):
        parts[part] = (tiles_ref[pl.ds(size * part, size), :] + tiles_ref[pl.ds(size * (part + 2), size), :]).T
        copy.start()
    for copy in copies:
        copy.wait()


def exchange(rows):
    groups = [tile_order(lax.axis_size("tile"))]
    moved = lax.all_to_all(rows[:, None, :], "tile", 0, 0, axis_index_groups=groups, tiled=True)
    return moved[:, 0, :]


def of_both_cores(rows):
    return lax.all_gather(rows, "dist", axis=0, tiled=True, axis_index_groups=[[0, 1], [2, 3]])


def body(object_re, object_im, intensity, shrink, offset, fresnel):
    size = object_re.shape[0]
    vmem = pl.BlockSpec(memory_space=pltpu.VMEM)
    phase = fresnel_phase(fresnel[0], size)
    columns = pl.pallas_call(
        partial(pack_kernel, size),
        out_shape=jax.ShapeDtypeStruct((2 * size, size), F32),
        in_specs=[pl.BlockSpec(memory_space=pl.ANY)] * 3,
        out_specs=vmem,
        scratch_shapes=[pltpu.VMEM((2, size, size), F32), pltpu.SemaphoreType.DMA((2,))],
        name="pack",
    )(object_re, object_im, intensity[0])
    field = of_both_cores(exchange(columns))
    gradient = run_column(jnp.concatenate([shrink, offset]), field, phase, size)
    first, second = of_both_cores(gradient).reshape(2, 2, size, size)
    own = jnp.where(core_index() == 0, first[0] + second[0], first[1] + second[1])
    tiles = lax.all_gather(exchange(own), "dist", axis=0, tiled=True)
    out = jax.ShapeDtypeStruct((size, size), F32)
    return pl.pallas_call(
        partial(finish_kernel, size),
        out_shape=(out, out),
        in_specs=[vmem],
        out_specs=(pl.BlockSpec(memory_space=pl.ANY),) * 2,
        scratch_shapes=[pltpu.VMEM((2, size, size), F32), pltpu.SemaphoreType.DMA((2,))],
        compiler_params=pltpu.CompilerParams(vmem_limit_bytes=8 * 1024 * 1024),
        name="finish",
    )(tiles)


def solution(mesh):
    in_specs = (
        P("tile", None),
        P("tile", None),
        P("dist", "tile", None),
        P("dist"),
        P("dist"),
        P("dist"),
    )
    out_specs = (P("tile", None), P("tile", None))
    return jax.shard_map(body, mesh=mesh, in_specs=in_specs, out_specs=out_specs, check_vma=False)
```

```python
from functools import partial
import math

import jax
import jax.numpy as jnp
import numpy as np
from jax import lax
from jax.experimental import pallas as pl
from jax.experimental.pallas import tpu as pltpu
from jax.sharding import PartitionSpec as P

F32 = jnp.float32
BF16 = jnp.bfloat16
LAYERS = 16


def two_terms(values):
    high = values.astype(BF16)
    low = (values - high.astype(np.float32)).astype(BF16)
    return high, low


def place_of(index, inner):
    return (index + 3 * inner // 4) % inner


def layer_slots():
    near = [0, 15, 14, 13, 12]
    order = [11, 10, 9, 1, 8, 2, 7, 3, 6, 4, 5] + near
    return [order.index(layer) for layer in range(LAYERS)]


def tile_order(size):
    inner = size // LAYERS
    layers = sorted(range(LAYERS), key=layer_slots().__getitem__)
    return [place_of(index, inner) * LAYERS + layer for layer in layers for index in range(inner)]


def constant_tables(size):
    index = np.arange(size, dtype=np.int64)
    product = np.outer(index, index)
    angle = 2.0 * np.pi / size * (product % size)
    real, imag = np.cos(angle), -np.sin(angle)
    inner = size // LAYERS
    tile = place_of(index % inner, inner) * LAYERS + index // inner
    tables = []
    for order in (tile, index):
        part, other = real[:, order], imag[:, order]
        block = np.block([[part, -other], [other, part]]).astype(np.float32)
        tables += two_terms(block) + two_terms(block.T)
    angle = 2.0 * np.pi / (size * size) * product
    twiddle = np.stack([np.cos(angle), -np.sin(angle)]).astype(np.float32)
    return np.concatenate(tables), twiddle


def split(values):
    high = values.astype(BF16)
    return high, (values - high.astype(F32)).astype(BF16)


def product(left, right):
    dot = partial(jnp.dot, preferred_element_type=F32)
    return dot(left[0], right[0]) + (dot(left[0], right[1]) + dot(left[1], right[0]))


def matmul(left, right):
    return jnp.dot(left, right, preferred_element_type=F32)


def times(first, second):
    return (
        first[0] * second[0] - first[1] * second[1],
        first[0] * second[1] + first[1] * second[0],
    )


def conj(pair):
    return (pair[0], -pair[1])


def propagate(values, tables, twiddle, kernel, size):
    rows, rows_t, lanes, lanes_t = tables

    def by_rows(table, pair):
        high, low = split(jnp.concatenate(pair, axis=0))
        out = matmul(table[0], jnp.concatenate([high, low], axis=1))
        out = out[:, :size] + (out[:, size:] + matmul(table[1], high))
        return (out[:size], out[size:])

    def by_lanes(pair, table):
        high, low = split(jnp.concatenate(pair, axis=1))
        out = matmul(jnp.concatenate([high, low], axis=0), table[0])
        out = out[:size] + (out[size:] + matmul(high, table[1]))
        return (out[:, :size], out[:, size:])

    mixed = times(by_rows(rows, values), twiddle)
    spectrum = times(by_lanes(mixed, lanes_t), kernel)
    mixed = times(by_lanes(spectrum, lanes), conj(twiddle))
    return by_rows(rows_t, mixed)


def column_kernel(size, scalars, field_ref, phase_ref, table_ref, twiddle_ref, out_ref):
    shape = (size, size)
    inner = size // LAYERS
    slots = layer_slots()
    line = lax.broadcasted_iota(jnp.int32, shape, 0)
    row = place_of(line % inner, inner) * LAYERS + line // inner
    lane = lax.broadcasted_iota(jnp.int32, shape, 1)
    total = size * size
    bits = total.bit_length() - 1
    shrink, offset = scalars[0], scalars[1]

    def scaled(index):
        centre = total // 2
        return centre * total + (index - centre) * (total - shrink) + offset * total

    position = scaled(row * size + lane)
    weight = jnp.bitwise_and(position, total - 1).astype(F32) * (1.0 / total)
    shift = lax.shift_right_arithmetic(scaled(row * size), bits) - row * size
    leading = lax.shift_right_arithmetic(position, bits) - (row * size + lane) == shift
    rest = 1.0 - weight

    place = place_of(lax.broadcasted_iota(jnp.int32, (inner, size), 0), inner)

    def rows_up(values):
        edge = pltpu.roll(values[:inner], inner - 1, 0)
        return jnp.concatenate([values[inner:], jnp.where(place == inner - 1, 0.0, edge)], axis=0)

    def rows_down(values):
        edge = pltpu.roll(values[size - inner :], 1, 0)
        return jnp.concatenate([jnp.where(place == 0, 0.0, edge), values[: size - inner]], axis=0)

    def lanes(values, index):
        return jnp.take_along_axis(values, jnp.bitwise_and(index, size - 1), axis=1, mode="promise_in_bounds")

    lower = row * size + lane + jnp.where(leading, shift, shift - 1)

    def sample(values):
        below, above = rows_down(values), rows_up(values)

        def window(first):
            return jnp.where(lane < first, above, jnp.where(lane >= first + size, below, values))

        return rest * lanes(window(shift), lower) + weight * lanes(window(shift + 1), lower + 1)

    def spread(values):
        near, far = rest * values, weight * values
        stay = up = down = 0.0
        for by, part in (
            (shift, jnp.where(leading, near, far)),
            (shift - 1, jnp.where(leading, 0.0, near)),
            (shift + 1, jnp.where(leading, far, 0.0)),
        ):
            moved = lanes(part, lane - by)
            to_next = lane < by
            to_last = lane >= by + size
            down += jnp.where(to_next, moved, 0.0)
            up += jnp.where(to_last, moved, 0.0)
            stay += jnp.where(jnp.logical_or(to_next, to_last), 0.0, moved)
        return stay + rows_down(down) + rows_up(up)

    def gathered(start):
        pieces = [field_ref[pl.ds(start + 2 * inner * slot, inner, stride=2), :] for slot in slots]
        return jnp.concatenate(pieces, axis=0)

    span = 2 * size
    terms = [table_ref[pl.ds(span * term, span), :] for term in range(8)]
    tables = [(terms[2 * term], terms[2 * term + 1]) for term in range(4)]
    twiddle = (twiddle_ref[0], twiddle_ref[1])
    kernel = (phase_ref[0], phase_ref[1])
    measured = jnp.where(core_index() == 0, gathered(1), gathered(span + 1))
    wave = propagate((sample(gathered(0)), sample(gathered(span))), tables, twiddle, kernel, size)
    power = wave[0] * wave[0] + wave[1] * wave[1]
    kept = 1.0 - jnp.sqrt(measured) * lax.rsqrt(jnp.maximum(power, 0.01))
    residual = (kept * wave[0], kept * wave[1])
    back = propagate(residual, tables, twiddle, conj(kernel), size)
    for part in range(2):
        result = spread(back[part])
        for layer, slot in enumerate(slots):
            start = size * part + inner * slot
            out_ref[start : start + inner, :] = result[inner * layer : inner * (layer + 1)]


def fresnel_phase(fresnel_now, size):
    total = size * size
    period = 64 * total
    index = jnp.arange(size, dtype=jnp.int32)
    frequency = index[:, None] + size * index[None, :]
    signed = jnp.where(frequency < total // 2, frequency, frequency - total)
    turns = fresnel_now * (signed * signed % period) % period
    theta = 2.0 * math.pi / period * turns.astype(F32)
    return jnp.stack([jnp.cos(theta), -jnp.sin(theta)]) * (1.0 / total)


def run_column(scalars, field, phase, size, **options):
    tables, twiddle = constant_tables(size)
    vmem = pl.BlockSpec(memory_space=pltpu.VMEM)
    return pl.pallas_call(
        partial(column_kernel, size),
        out_shape=jax.ShapeDtypeStruct((2 * size, size), F32),
        in_specs=[pl.BlockSpec(memory_space=pltpu.SMEM)] + [vmem] * 4,
        out_specs=vmem,
        compiler_params=pltpu.CompilerParams(vmem_limit_bytes=16 * 1024 * 1024),
        name="column",
        **options,
    )(
        scalars,
        field,
        phase,
        jnp.asarray(tables),
        jnp.asarray(twiddle),
    )


def core_index():
    return jnp.bitwise_and(lax.axis_index("dist"), 1)


def pack_kernel(size, re_ref, im_ref, intensity_ref, out_ref, tiles, arrived):
    copies = [pltpu.make_async_copy(intensity_ref, tiles.at[1], arrived.at[1])]
    for core, ref in enumerate((re_ref, im_ref)):
        copies.append(pltpu.make_async_copy(ref, tiles.at[0], arrived.at[0]))
        pl.when(core_index() == core)(copies[-1].start)
    copies[0].start()
    copies[1].wait()
    out_ref[pl.ds(0, size, stride=2), :] = tiles[0].T
    copies[0].wait()
    out_ref[pl.ds(1, size, stride=2), :] = tiles[1].T


def finish_kernel(size, tiles_ref, re_ref, im_ref):
    for part, ref in enumerate((re_ref, im_ref)):
        ref[...] = (tiles_ref[pl.ds(size * part, size), :] + tiles_ref[pl.ds(size * (part + 2), size), :]).T


def exchange(rows):
    groups = [tile_order(lax.axis_size("tile"))]
    moved = lax.all_to_all(rows[:, None, :], "tile", 0, 0, axis_index_groups=groups, tiled=True)
    return moved[:, 0, :]


def of_both_cores(rows):
    return lax.all_gather(rows, "dist", axis=0, tiled=True, axis_index_groups=[[0, 1], [2, 3]])


def body(object_re, object_im, intensity, shrink, offset, fresnel):
    size = object_re.shape[0]
    vmem = pl.BlockSpec(memory_space=pltpu.VMEM)
    phase = fresnel_phase(fresnel[0], size)
    columns = pl.pallas_call(
        partial(pack_kernel, size),
        out_shape=jax.ShapeDtypeStruct((2 * size, size), F32),
        in_specs=[pl.BlockSpec(memory_space=pl.ANY)] * 3,
        out_specs=vmem,
        scratch_shapes=[pltpu.VMEM((2, size, size), F32), pltpu.SemaphoreType.DMA((2,))],
        name="pack",
    )(object_re, object_im, intensity[0])
    field = of_both_cores(exchange(columns))
    gradient = run_column(jnp.concatenate([shrink, offset]), field, phase, size)
    first, second = of_both_cores(gradient).reshape(2, 2, size, size)
    own = jnp.where(core_index() == 0, first[0] + second[0], first[1] + second[1])
    tiles = lax.all_gather(exchange(own), "dist", axis=0, tiled=True)
    out = jax.ShapeDtypeStruct((size, size), F32)
    return pl.pallas_call(
        partial(finish_kernel, size),
        out_shape=(out, out),
        in_specs=[vmem],
        out_specs=(vmem, vmem),
        compiler_params=pltpu.CompilerParams(vmem_limit_bytes=8 * 1024 * 1024),
        name="finish",
    )(tiles)


def solution(mesh):
    in_specs = (
        P("tile", None),
        P("tile", None),
        P("dist", "tile", None),
        P("dist"),
        P("dist"),
        P("dist"),
    )
    out_specs = (P("tile", None), P("tile", None))
    return jax.shard_map(body, mesh=mesh, in_specs=in_specs, out_specs=out_specs, check_vma=False)
```

```python
from functools import partial
import math

import jax
import jax.numpy as jnp
import numpy as np
from jax import lax
from jax.experimental import pallas as pl
from jax.experimental.pallas import tpu as pltpu
from jax.sharding import PartitionSpec as P

F32 = jnp.float32
BF16 = jnp.bfloat16
LAYERS = 16


def two_terms(values):
    high = values.astype(BF16)
    low = (values - high.astype(np.float32)).astype(BF16)
    return high, low


def place_of(index, inner):
    return (index + 3 * inner // 4) % inner


def layer_slots():
    near = [0, 15, 14, 13, 12]
    order = [10, 9, 1, 8, 2, 7, 3, 6, 4, 5] + near + [11]
    return [order.index(layer) for layer in range(LAYERS)]


def tile_order(size):
    inner = size // LAYERS
    layers = sorted(range(LAYERS), key=layer_slots().__getitem__)
    return [place_of(index, inner) * LAYERS + layer for layer in layers for index in range(inner)]


def constant_tables(size):
    index = np.arange(size, dtype=np.int64)
    product = np.outer(index, index)
    angle = 2.0 * np.pi / size * (product % size)
    real, imag = np.cos(angle), -np.sin(angle)
    inner = size // LAYERS
    tile = place_of(index % inner, inner) * LAYERS + index // inner
    tables = []
    for order in (tile, index):
        part, other = real[:, order], imag[:, order]
        block = np.block([[part, -other], [other, part]]).astype(np.float32)
        tables += two_terms(block) + two_terms(block.T)
    angle = 2.0 * np.pi / (size * size) * product
    twiddle = np.stack([np.cos(angle), -np.sin(angle)]).astype(np.float32)
    return np.concatenate(tables), twiddle


def split(values):
    high = values.astype(BF16)
    return high, (values - high.astype(F32)).astype(BF16)


def product(left, right):
    dot = partial(jnp.dot, preferred_element_type=F32)
    return dot(left[0], right[0]) + (dot(left[0], right[1]) + dot(left[1], right[0]))


def matmul(left, right):
    return jnp.dot(left, right, preferred_element_type=F32)


def times(first, second):
    return (
        first[0] * second[0] - first[1] * second[1],
        first[0] * second[1] + first[1] * second[0],
    )


def conj(pair):
    return (pair[0], -pair[1])


def propagate(values, tables, twiddle, kernel, size):
    rows, rows_t, lanes, lanes_t = tables

    def by_rows(table, pair):
        high, low = split(jnp.concatenate(pair, axis=0))
        out = matmul(table[0], jnp.concatenate([high, low], axis=1))
        out = out[:, :size] + (out[:, size:] + matmul(table[1], high))
        return (out[:size], out[size:])

    def by_lanes(pair, table):
        high, low = split(jnp.concatenate(pair, axis=1))
        out = matmul(jnp.concatenate([high, low], axis=0), table[0])
        out = out[:size] + (out[size:] + matmul(high, table[1]))
        return (out[:, :size], out[:, size:])

    mixed = times(by_rows(rows, values), twiddle)
    spectrum = times(by_lanes(mixed, lanes_t), kernel)
    mixed = times(by_lanes(spectrum, lanes), conj(twiddle))
    return by_rows(rows_t, mixed)


def column_kernel(size, scalars, field_ref, phase_ref, table_ref, twiddle_ref, out_ref):
    shape = (size, size)
    inner = size // LAYERS
    slots = layer_slots()
    line = lax.broadcasted_iota(jnp.int32, shape, 0)
    row = place_of(line % inner, inner) * LAYERS + line // inner
    lane = lax.broadcasted_iota(jnp.int32, shape, 1)
    total = size * size
    bits = total.bit_length() - 1
    shrink, offset = scalars[0], scalars[1]

    def scaled(index):
        centre = total // 2
        return centre * total + (index - centre) * (total - shrink) + offset * total

    position = scaled(row * size + lane)
    weight = jnp.bitwise_and(position, total - 1).astype(F32) * (1.0 / total)
    shift = lax.shift_right_arithmetic(scaled(row * size), bits) - row * size
    leading = lax.shift_right_arithmetic(position, bits) - (row * size + lane) == shift
    rest = 1.0 - weight

    place = place_of(lax.broadcasted_iota(jnp.int32, (inner, size), 0), inner)

    def rows_up(values):
        edge = pltpu.roll(values[:inner], inner - 1, 0)
        return jnp.concatenate([values[inner:], jnp.where(place == inner - 1, 0.0, edge)], axis=0)

    def rows_down(values):
        edge = pltpu.roll(values[size - inner :], 1, 0)
        return jnp.concatenate([jnp.where(place == 0, 0.0, edge), values[: size - inner]], axis=0)

    def lanes(values, index):
        return jnp.take_along_axis(values, jnp.bitwise_and(index, size - 1), axis=1, mode="promise_in_bounds")

    lower = row * size + lane + jnp.where(leading, shift, shift - 1)

    def sample(values):
        below, above = rows_down(values), rows_up(values)

        def window(first):
            return jnp.where(lane < first, above, jnp.where(lane >= first + size, below, values))

        return rest * lanes(window(shift), lower) + weight * lanes(window(shift + 1), lower + 1)

    def spread(values):
        near, far = rest * values, weight * values
        stay = up = down = 0.0
        for by, part in (
            (shift, jnp.where(leading, near, far)),
            (shift - 1, jnp.where(leading, 0.0, near)),
            (shift + 1, jnp.where(leading, far, 0.0)),
        ):
            moved = lanes(part, lane - by)
            to_next = lane < by
            to_last = lane >= by + size
            down += jnp.where(to_next, moved, 0.0)
            up += jnp.where(to_last, moved, 0.0)
            stay += jnp.where(jnp.logical_or(to_next, to_last), 0.0, moved)
        return stay + rows_down(down) + rows_up(up)

    def gathered(start):
        pieces = [field_ref[pl.ds(start + 2 * inner * slot, inner, stride=2), :] for slot in slots]
        return jnp.concatenate(pieces, axis=0)

    span = 2 * size
    terms = [table_ref[pl.ds(span * term, span), :] for term in range(8)]
    tables = [(terms[2 * term], terms[2 * term + 1]) for term in range(4)]
    twiddle = (twiddle_ref[0], twiddle_ref[1])
    kernel = (phase_ref[0], phase_ref[1])
    measured = jnp.where(core_index() == 0, gathered(1), gathered(span + 1))
    wave = propagate((sample(gathered(0)), sample(gathered(span))), tables, twiddle, kernel, size)
    power = wave[0] * wave[0] + wave[1] * wave[1]
    kept = 1.0 - jnp.sqrt(measured) * lax.rsqrt(jnp.maximum(power, 0.01))
    residual = (kept * wave[0], kept * wave[1])
    back = propagate(residual, tables, twiddle, conj(kernel), size)
    for part in range(2):
        result = spread(back[part])
        for layer, slot in enumerate(slots):
            start = size * part + inner * slot
            out_ref[start : start + inner, :] = result[inner * layer : inner * (layer + 1)]


def fresnel_phase(fresnel_now, size):
    total = size * size
    period = 64 * total
    index = jnp.arange(size, dtype=jnp.int32)
    frequency = index[:, None] + size * index[None, :]
    signed = jnp.where(frequency < total // 2, frequency, frequency - total)
    turns = fresnel_now * (signed * signed % period) % period
    theta = 2.0 * math.pi / period * turns.astype(F32)
    return jnp.stack([jnp.cos(theta), -jnp.sin(theta)]) * (1.0 / total)


def run_column(scalars, field, phase, size, **options):
    tables, twiddle = constant_tables(size)
    vmem = pl.BlockSpec(memory_space=pltpu.VMEM)
    return pl.pallas_call(
        partial(column_kernel, size),
        out_shape=jax.ShapeDtypeStruct((2 * size, size), F32),
        in_specs=[pl.BlockSpec(memory_space=pltpu.SMEM)] + [vmem] * 4,
        out_specs=vmem,
        compiler_params=pltpu.CompilerParams(vmem_limit_bytes=16 * 1024 * 1024),
        name="column",
        **options,
    )(
        scalars,
        field,
        phase,
        jnp.asarray(tables),
        jnp.asarray(twiddle),
    )


def core_index():
    return jnp.bitwise_and(lax.axis_index("dist"), 1)


def pack_kernel(size, re_ref, im_ref, intensity_ref, out_ref, tiles, arrived):
    copies = [pltpu.make_async_copy(intensity_ref, tiles.at[1], arrived.at[1])]
    for core, ref in enumerate((re_ref, im_ref)):
        copies.append(pltpu.make_async_copy(ref, tiles.at[0], arrived.at[0]))
        pl.when(core_index() == core)(copies[-1].start)
    copies[0].start()
    copies[1].wait()
    out_ref[pl.ds(0, size, stride=2), :] = tiles[0].T
    copies[0].wait()
    out_ref[pl.ds(1, size, stride=2), :] = tiles[1].T


def finish_kernel(size, tiles_ref, re_ref, im_ref):
    for part, ref in enumerate((re_ref, im_ref)):
        ref[...] = (tiles_ref[pl.ds(size * part, size), :] + tiles_ref[pl.ds(size * (part + 2), size), :]).T


def exchange(rows):
    groups = [tile_order(lax.axis_size("tile"))]
    moved = lax.all_to_all(rows[:, None, :], "tile", 0, 0, axis_index_groups=groups, tiled=True)
    return moved[:, 0, :]


def of_both_cores(rows):
    return lax.all_gather(rows, "dist", axis=0, tiled=True, axis_index_groups=[[0, 1], [2, 3]])


def body(object_re, object_im, intensity, shrink, offset, fresnel):
    size = object_re.shape[0]
    vmem = pl.BlockSpec(memory_space=pltpu.VMEM)
    phase = fresnel_phase(fresnel[0], size)
    columns = pl.pallas_call(
        partial(pack_kernel, size),
        out_shape=jax.ShapeDtypeStruct((2 * size, size), F32),
        in_specs=[pl.BlockSpec(memory_space=pl.ANY)] * 3,
        out_specs=vmem,
        scratch_shapes=[pltpu.VMEM((2, size, size), F32), pltpu.SemaphoreType.DMA((2,))],
        name="pack",
    )(object_re, object_im, intensity[0])
    field = of_both_cores(exchange(columns))
    gradient = run_column(jnp.concatenate([shrink, offset]), field, phase, size)
    first, second = of_both_cores(gradient).reshape(2, 2, size, size)
    own = jnp.where(core_index() == 0, first[0] + second[0], first[1] + second[1])
    tiles = lax.all_gather(exchange(own), "dist", axis=0, tiled=True)
    out = jax.ShapeDtypeStruct((size, size), F32)
    return pl.pallas_call(
        partial(finish_kernel, size),
        out_shape=(out, out),
        in_specs=[vmem],
        out_specs=(vmem, vmem),
        compiler_params=pltpu.CompilerParams(vmem_limit_bytes=8 * 1024 * 1024),
        name="finish",
    )(tiles)


def solution(mesh):
    in_specs = (
        P("tile", None),
        P("tile", None),
        P("dist", "tile", None),
        P("dist"),
        P("dist"),
        P("dist"),
    )
    out_specs = (P("tile", None), P("tile", None))
    return jax.shard_map(body, mesh=mesh, in_specs=in_specs, out_specs=out_specs, check_vma=False)
```
